256 devices in a mesh: head: 16 (over z, x_hi), ctx: 16 (over y, x_lo, core).
Axes of the slice: x: 4 (x_hi: 2, x_lo: 2; x = x_hi * 2 + x_lo), y: 4, z: 8, core: 2. Of those that a mesh axis runs over, the one named last changes fastest.
Arguments:
- queries: bfloat16 [32768, 2048], P(('head', 'ctx')), may hold values from -16 to 16
- keys: bfloat16 [32768, 256], P(('head', 'ctx')), may hold values from -16 to 16
- values: bfloat16 [32768, 256], P(('head', 'ctx')), may hold values from -6 to 6
- lengths: int32 [16], replicated, may hold values from 1 to 384, 512 in all
Outputs:
- attended: bfloat16 [32768, 2048], P(('head', 'ctx'))
The draws below stay inside these ranges and needn't reach their ends.
All inputs are finite; a program needn't handle non-finite values.
Results may differ from the reference program's by a relative error of at most 0.006.
Values may be sent and summed in bfloat16 or wider, within the bound.
No kernel may reach another device: no remote copies, remote signals or barrier semaphores. Data moves between devices by JAX's collectives and lax.ppermute only.
A program may use at most 64 MiB of HBM per device.

```python
import math
import jax
import jax.numpy as jnp
import numpy as np
from jax import lax

QH = 16
KVH = 2
HD = 128
BLOCK = 64
NDOC = 16
LEN = 32768
NBLK = 512


def draw_keys(key, part):
    key = jax.random.fold_in(key, 3)
    drawn = jax.random.normal(key, (LEN, KVH * HD), jnp.float32)
    return drawn.astype(jnp.bfloat16)


def draw_queries(key, part):
    key = jax.random.fold_in(key, 5)
    drawn = jax.random.normal(key, (LEN, QH * HD), jnp.float32)
    return drawn.astype(jnp.bfloat16)


def shard_levels(rng, dims, cuts, smallest, high):
    def one(position, parts):
        heights = jax.random.uniform(jax.random.fold_in(jax.random.fold_in(rng, 6), position), (parts,), jnp.float32, smallest / len(cuts), high / len(cuts))
        return jnp.repeat(jnp.exp(heights), dims[position] // parts).reshape((-1,) + (1,) * (len(dims) - position - 1))

    gain = one(*cuts[0])
    for cut in cuts[1:]:
        gain = gain * one(*cut)
    return gain


def split_up(count, total, bound, slope):
    portions = [(1 << 20) // math.isqrt(standing ** slope) + 1 for standing in range(2, count + 1)]
    rest, counts = total - bound - (count - 1), [1] * (count - 1)
    while rest > 0:
        free = [i for i in range(count - 1) if counts[i] < bound]
        pool, remaining = sum([portions[i] for i in free]), rest
        for i in free:
            extra = min(bound - counts[i], max(1, remaining * portions[i] // pool), rest)
            counts[i] = counts[i] + extra
            rest = rest - extra
    return np.array([bound] + counts)


def uneven_parts(key, number_of, total, bound, lean):
    if number_of == 2:
        one = jax.random.randint(key, (), max(1, total - bound), min(bound, total - 1) + 1)
        return jnp.stack([one, total - one])
    sizes = jnp.asarray(split_up(number_of, total, bound, lean), jnp.int32)
    twos = (number_of - 1) // 2
    donor, taker = sizes[1:1 + 2 * twos:2], sizes[2:2 + 2 * twos:2]
    room = jnp.minimum(donor - 1, bound - taker)
    moved = jax.random.randint(jax.random.fold_in(key, 1), (twos,), 0, 1 << 20) % (room + 1)
    sizes = sizes.at[1:1 + 2 * twos:2].set(donor - moved).at[2:2 + 2 * twos:2].set(taker + moved)
    return sizes[jax.random.permutation(jax.random.fold_in(key, 2), number_of)]


def normal_values(stream_key, extent, scale, reach, split=(), kind=jnp.bfloat16):
    values = jax.random.normal(stream_key, extent, jnp.float32) * scale
    if len(split) > 0:
        values = shard_levels(stream_key, extent, split, -0.22, 0.18) * values
    return jnp.clip(values, min=-reach, max=reach).astype(kind)


def setup_inputs(seed: int = 0) -> dict:
    splits = jax.random.split(jax.random.key(seed), 5)
    queries = draw_queries(jax.random.fold_in(splits[4], 71), 0)
    keys = draw_keys(jax.random.fold_in(splits[4], 71), 0)
    values = normal_values(splits[2], (LEN, KVH * HD), 1.0, 6.0, ((0, 256),))
    lengths = uneven_parts(splits[3], NDOC, NBLK, NBLK * 3 // 4, 2).astype(jnp.int32)
    return dict(queries=queries, keys=keys, values=values, lengths=lengths)


def reference(queries, keys, values, lengths):
    doc_ends = jnp.cumsum(lengths).astype(jnp.int32) * BLOCK
    positions = jnp.arange(LEN, dtype=jnp.int32)
    doc_ids = jnp.sum((positions[:, None] >= doc_ends[None, :]).astype(jnp.int32), axis=1)
    group = QH // KVH
    q_rows = min(1024, LEN)
    blocks = LEN // q_rows
    scale = 1.0 / (HD ** 0.5)

    def head_out(head):
        kv_head = head // group
        q_head = lax.dynamic_slice_in_dim(queries, head * HD, HD, 1)
        k_head = lax.dynamic_slice_in_dim(keys, kv_head * HD, HD, 1)
        v_head = lax.dynamic_slice_in_dim(values, kv_head * HD, HD, 1)

        def one_block(index):
            start = (index * q_rows).astype(jnp.int32)
            q_part = lax.dynamic_slice_in_dim(q_head, start, q_rows, 0)
            q_pos = lax.dynamic_slice_in_dim(positions, start, q_rows, 0)
            q_doc = lax.dynamic_slice_in_dim(doc_ids, start, q_rows, 0)
            scores = jnp.dot(q_part, k_head.T, preferred_element_type=jnp.float32) * scale
            allowed = (doc_ids[None, :] == q_doc[:, None]) & (positions[None, :] <= q_pos[:, None])
            scores = jnp.where(allowed, scores, -jnp.inf)
            top = jnp.max(scores, axis=1, keepdims=True)
            expo = jnp.exp(scores - top)
            total = jnp.sum(expo, axis=1, keepdims=True)
            weights = expo.astype(jnp.bfloat16)
            return jnp.dot(weights, v_head, preferred_element_type=jnp.float32) / total

        result = lax.map(one_block, jnp.arange(blocks, dtype=jnp.int32))
        return result.reshape(LEN, HD).astype(jnp.bfloat16)

    stacked = lax.map(head_out, jnp.arange(QH, dtype=jnp.int32))
    return jnp.transpose(stacked, (1, 0, 2)).reshape(LEN, QH * HD)
```

```python
import functools
import math

import jax
import jax.numpy as jnp
from jax import lax
from jax.experimental import pallas as pl
from jax.experimental.pallas import tpu as pltpu
from jax.sharding import Mesh, PartitionSpec as P

HD = 128
BLOCK = 64
AXES = ("z", "xh", "y", "xl", "c")
SIZES = (8, 2, 4, 2, 2)
PLANE = 4096
TILE = 128
MASKED = -2e30
FLOOR = -1e29
LOG2E_SCALE = math.log2(math.e) / math.sqrt(HD)
RC = 8
WIDE = RC * TILE
SPAN = 2 * WIDE
PER = PLANE // SPAN


def attend_kernel(info, q_own, q_other, kv, o_own, o_other, lse_own, lse_other,
                  qq, acc, peak, total, score, weight, top, fade, units):
    place = info[0]
    core = info[1]
    for half, ref in enumerate((q_own, q_other)):
        for head in range(2):
            full = ref[:, head].astype(jnp.float32) * LOG2E_SCALE
            high = full.astype(jnp.bfloat16)
            lanes = slice(head * 256 + half * 128, head * 256 + half * 128 + 128)
            qq[:, :HD, lanes] = high
            qq[:, HD:, lanes] = (full - high.astype(jnp.float32)).astype(jnp.bfloat16)
    acc[...] = jnp.zeros_like(acc)
    total[...] = jnp.zeros_like(total)
    peak[...] = jnp.full_like(peak, FLOOR)

    def keys_of(n):
        return kv[pl.ds((n % PER) * RC, RC), n // PER]

    def bounds(z):
        lane = lax.broadcasted_iota(jnp.int32, (1, 512), 1) % 256
        b = lane // 64
        at = 4 + z * 6
        start = jnp.where(b == 0, info[at], jnp.where(b == 1, info[at + 1],
                          jnp.where(b == 2, info[at + 2], info[at + 3])))
        part = jnp.where(lane < 128, core, 1 - core) * 128
        return start, z * PLANE + place + part + lane % 128

    def scores_of(z, n, masked):
        k = keys_of(n)[:, :, :HD].reshape(WIDE, HD)
        s = jnp.dot(jnp.concatenate([k, k], axis=1), qq[z], preferred_element_type=jnp.float32)
        if masked:
            start, stop = bounds(z)
            row = lax.broadcasted_iota(jnp.int32, (TILE, 512), 0)
            parts = []
            for g in range(RC):
                base = n * SPAN + g * 256 + core * TILE
                keep = (row >= start - base) & (row <= stop - base)
                parts.append(jnp.where(keep, s[g * TILE:(g + 1) * TILE], MASKED))
            s = jnp.concatenate(parts, axis=0)
        score[...] = s
        top[...] = jnp.max(s.reshape(WIDE // 8, 8, 512), axis=0)

    def weigh(z):
        old = peak[z]
        new = jnp.maximum(old, jnp.max(top[...], axis=0, keepdims=True))
        factor = jnp.exp2(old - new)
        fade[...] = factor
        peak[z] = new
        sums = total[z] * factor
        for u in range(WIDE // 16):
            rows = slice(u * 16, u * 16 + 16)
            p = jnp.exp2(score[rows, :].reshape(2, 8, 512) - new)
            sums = sums + (p[0] + p[1])
            weight[rows, :] = p.reshape(16, 512).astype(jnp.bfloat16)
        total[z] = sums

    def gather(z, n):
        v = keys_of(n)[:, :, HD:]
        pv = jnp.dot(jnp.concatenate([v[g] for g in range(RC)], axis=1), weight[...],
                     preferred_element_type=jnp.float32)
        acc[z] = (acc[z].reshape(16, 8, 512) * fade[...] + pv.reshape(16, 8, 512)).reshape(HD, 512)

    def run(masked):
        def build(z, count):
            first = info[4 + z * 6 + 4] // SPAN
            last = (z * PLANE + place) // SPAN
            clear = jnp.minimum((info[4 + z * 6 + 5] + SPAN - 1) // SPAN, last)

            def put(n, count):
                units[count] = z * 256 + n
                return count + 1

            if masked:
                return lax.fori_loop(first, clear, put, put(last, count))
            return lax.fori_loop(clear, last, put, count)

        count = lax.fori_loop(0, 8, build, 0)

        def at(i):
            return units[i] // 256, units[i] % 256

        @pl.when(count > 0)
        def _():
            scores_of(*at(0), masked)
            weight[...] = jnp.zeros_like(weight)
            fade[...] = jnp.ones_like(fade)

            def body(i, carry):
                z, n = at(i)
                gather(*at(jnp.maximum(i - 1, 0)))
                weigh(z)
                scores_of(*at(jnp.minimum(i + 1, count - 1)), masked)
                return carry

            lax.fori_loop(0, count, body, 0)
            gather(*at(count - 1))

    run(True)
    run(False)
    for z in range(8):
        l = jnp.sum(total[z], axis=0, keepdims=True)
        o = acc[z] / jnp.where(l > 0, l, 1.0)
        lse = jnp.where(l > 0, peak[z, :1] + jnp.log2(jnp.where(l > 0, l, 1.0)), FLOOR)
        for head in range(2):
            for half, (o_ref, lse_ref) in enumerate(((o_own, lse_own), (o_other, lse_other))):
                lanes = slice(head * 256 + half * 128, head * 256 + half * 128 + 128)
                o_ref[z, head] = o[:, lanes].astype(o_ref.dtype)
                lse_ref[z, head] = jnp.broadcast_to(lse[:, lanes], (8, TILE))


def attend(info, q_own, q_other, kv):
    vmem = pltpu.VMEM
    f32, bf16 = jnp.float32, jnp.bfloat16
    o = jax.ShapeDtypeStruct((8, 2, HD, TILE), bf16)
    lse = jax.ShapeDtypeStruct((8, 2, 8, TILE), f32)
    return pl.pallas_call(
        attend_kernel,
        out_shape=(o, o, lse, lse),
        in_specs=[pl.BlockSpec(memory_space=pltpu.SMEM)] + [pl.BlockSpec(memory_space=vmem)] * 3,
        out_specs=[pl.BlockSpec(memory_space=vmem)] * 4,
        scratch_shapes=[
            vmem((8, 2 * HD, 512), bf16),
            vmem((8, HD, 512), f32),
            vmem((8, 8, 512), f32),
            vmem((8, 8, 512), f32),
            vmem((WIDE, 512), f32),
            vmem((WIDE, 512), bf16),
            vmem((8, 512), f32),
            vmem((8, 512), f32),
            pltpu.SMEM((8 * PER * 8 + 16,), jnp.int32),
        ],
        compiler_params=pltpu.CompilerParams(vmem_limit_bytes=48 * 2**20),
    )(info, q_own, q_other, kv)


def positions(lengths):
    core = lax.axis_index("c")
    place = (lax.axis_index("xh") * 8 + lax.axis_index("y") * 2 + lax.axis_index("xl")) * 256
    ends = jnp.cumsum(lengths) * BLOCK
    b = jnp.arange(4, dtype=jnp.int32)
    own_first = jnp.where(b < 2, core, 1 - core) * 128 + (b % 2) * 64
    offsets = jnp.concatenate([own_first, jnp.array([0, 192], jnp.int32)])
    tokens = jnp.arange(8, dtype=jnp.int32)[:, None] * PLANE + place + offsets[None, :]
    starts = jnp.max(jnp.where(ends[None, None, :] <= tokens[:, :, None], ends[None, None, :], 0), axis=2)
    head = jnp.stack([place, core, core, core])
    return jnp.concatenate([head, starts.reshape(48)]).astype(jnp.int32)


def shards(queries, keys, values, lengths):
    swap = [(0, 1), (1, 0)]
    k = keys.reshape(TILE, 2, HD).transpose(1, 0, 2)
    vt = values.reshape(TILE, 2, HD).transpose(1, 2, 0)
    kv = jnp.concatenate([k, vt], axis=2)
    kv_send = jnp.repeat(kv, 4, axis=0)
    kv_z = lax.all_to_all(kv_send, "z", split_axis=0, concat_axis=0, tiled=True)
    kv_all = lax.all_gather(kv_z, ("xh", "y", "xl"), axis=0, tiled=False)
    qt = queries.reshape(TILE, 8, 2, HD).transpose(1, 2, 3, 0)
    q_own = lax.all_to_all(qt, "z", split_axis=0, concat_axis=0, tiled=True)
    q_other = lax.ppermute(q_own, "c", swap)
    info = positions(lengths)
    o_own, o_other, lse_own, lse_other = attend(info, q_own, q_other, kv_all.reshape(16, 8, TILE, 2 * HD))
    o_got = lax.ppermute(o_other, "c", swap)
    lse_got = lax.ppermute(lse_other, "c", swap)
    a, b = lse_own[:, :, :1], lse_got[:, :, :1]
    most = jnp.maximum(a, b)
    wa, wb = jnp.exp2(a - most), jnp.exp2(b - most)
    o = (o_own.astype(jnp.float32) * wa + o_got.astype(jnp.float32) * wb) / (wa + wb)
    back = lax.all_to_all(o.astype(jnp.bfloat16), "z", split_axis=0, concat_axis=0, tiled=True)
    return back.transpose(3, 0, 1, 2).reshape(TILE, 16 * HD)


def solution(mesh):
    fine = Mesh(mesh.devices.reshape(SIZES), AXES)
    spec = P(AXES, None)
    return jax.shard_map(
        shards, mesh=fine, in_specs=(spec, spec, spec, P()), out_specs=spec, check_vma=False
    )
```

```python
import functools
import math

import jax
import jax.numpy as jnp
from jax import lax
from jax.experimental import pallas as pl
from jax.experimental.pallas import tpu as pltpu
from jax.sharding import Mesh, PartitionSpec as P

HD = 128
BLOCK = 64
AXES = ("z", "xh", "y", "xl", "c")
SIZES = (8, 2, 4, 2, 2)
PLANE = 4096
TILE = 128
MASKED = -2e30
FLOOR = -1e29
LOG2E_SCALE = math.log2(math.e) / math.sqrt(HD)
SLOTS = ((0, 1, -1, 2), (-2, 3, -3, 4))
SHIFTS = (0, -1, 1, 2)


def attend_kernel(chunks, wide, first, last, moves, *refs):
    info, table = refs[:2]
    rest = list(refs[2:])
    if first:
        q_own, q_other = rest[:2]
        del rest[:2]
    else:
        state = rest[:4]
        del rest[:4]
    sources = rest[:len(moves)]
    del rest[:len(moves)]
    if first:
        qq = rest.pop(0)
    else:
        qq = state[0]
    if last:
        o_own, o_other, lse_own, lse_other = rest[:4]
        del rest[:4]
    acc, peak, total, kv, score, weight, top, fade, units, masked_units, sems = rest
    keys = wide * TILE

    copies = [pltpu.make_async_copy(src.at[a], kv.at[b], sems.at[i])
              for i, (src, (a, b)) in enumerate((s, m) for s, ms in zip(sources, moves) for m in ms)]
    for copy in copies:
        copy.start()
    place = info[0]
    core = info[1]
    if first:
        for half, ref in enumerate((q_own, q_other)):
            for head in range(2):
                full = ref[:, head].astype(jnp.float32) * LOG2E_SCALE
                high = full.astype(jnp.bfloat16)
                lanes = slice(head * 256 + half * 128, head * 256 + half * 128 + 128)
                qq[:, :HD, lanes] = high
                qq[:, HD:, lanes] = (full - high.astype(jnp.float32)).astype(jnp.bfloat16)
        acc[...] = jnp.zeros_like(acc)
        total[...] = jnp.zeros_like(total)
        peak[...] = jnp.full_like(peak, FLOOR)
    else:
        for ref, old in zip((acc, peak, total), state[1:]):
            ref[...] = old[...]

    def sort_out(e, counts):
        plain, masked = counts
        z, ch = e // chunks, e % chunks
        low, high = table[chunks * wide + ch], table[chunks * wide + chunks + ch]
        begin = z * PLANE + place
        need = (low <= begin + 255) & (high >= info[4 + z * 6 + 4])
        clear = (high <= begin) & (low >= info[4 + z * 6 + 5])
        units[plain] = e
        masked_units[masked] = e
        return (plain + jnp.where(need & clear, 1, 0), masked + jnp.where(need & ~clear, 1, 0))

    zero = jnp.int32(0)
    plain_count, masked_count = lax.fori_loop(0, 8 * chunks, sort_out, (zero, zero))
    for copy in copies:
        copy.wait()

    def bounds(z):
        lane = lax.broadcasted_iota(jnp.int32, (1, 512), 1) % 256
        b = lane // 64
        at = 4 + z * 6
        start = jnp.where(b == 0, info[at], jnp.where(b == 1, info[at + 1],
                          jnp.where(b == 2, info[at + 2], info[at + 3])))
        part = jnp.where(lane < 128, core, 1 - core) * 128
        return start, z * PLANE + place + part + lane % 128

    def scores_of(z, ch, masked):
        k = kv[ch, :, :, :HD].reshape(keys, HD)
        s = jnp.dot(jnp.concatenate([k, k], axis=1), qq[z], preferred_element_type=jnp.float32)
        if masked:
            start, stop = bounds(z)
            row = lax.broadcasted_iota(jnp.int32, (TILE, 512), 0)
            parts = []
            for g in range(wide):
                base = table[ch * wide + g]
                keep = (row >= start - base) & (row <= stop - base)
                parts.append(jnp.where(keep, s[g * TILE:(g + 1) * TILE], MASKED))
            s = jnp.concatenate(parts, axis=0)
        score[...] = s
        top[...] = jnp.max(s.reshape(keys // 8, 8, 512), axis=0)

    def weigh(z):
        old = peak[z]
        new = jnp.maximum(old, jnp.max(top[...], axis=0, keepdims=True))
        factor = jnp.exp2(old - new)
        fade[...] = factor
        peak[z] = new
        sums = total[z] * factor
        for u in range(keys // 16):
            rows = slice(u * 16, u * 16 + 16)
            p = jnp.exp2(score[rows, :].reshape(2, 8, 512) - new)
            sums = sums + (p[0] + p[1])
            weight[rows, :] = p.reshape(16, 512).astype(jnp.bfloat16)
        total[z] = sums

    def collect(z, ch):
        v = kv[ch, :, :, HD:]
        pv = jnp.dot(jnp.concatenate([v[g] for g in range(wide)], axis=1), weight[...],
                     preferred_element_type=jnp.float32)
        acc[z] = (acc[z].reshape(16, 8, 512) * fade[...] + pv.reshape(16, 8, 512)).reshape(HD, 512)

    def run(listed, count, masked):
        def at(i):
            return listed[i] // chunks, listed[i] % chunks

        @pl.when(count > 0)
        def _():
            scores_of(*at(0), masked)
            weight[...] = jnp.zeros_like(weight)
            fade[...] = jnp.ones_like(fade)

            def body(i, carry):
                z, _ = at(i)
                collect(*at(jnp.maximum(i - 1, 0)))
                weigh(z)
                scores_of(*at(jnp.minimum(i + 1, count - 1)), masked)
                return carry

            lax.fori_loop(0, count, body, 0)
            collect(*at(count - 1))

    run(masked_units, masked_count, True)
    run(units, plain_count, False)
    if last:
        for z in range(8):
            l = jnp.sum(total[z], axis=0, keepdims=True)
            o = acc[z] / jnp.where(l > 0, l, 1.0)
            lse = jnp.where(l > 0, peak[z, :1] + jnp.log2(jnp.where(l > 0, l, 1.0)), FLOOR)
            for head in range(2):
                for half, (o_ref, lse_ref) in enumerate(((o_own, lse_own), (o_other, lse_other))):
                    lanes = slice(head * 256 + half * 128, head * 256 + half * 128 + 128)
                    o_ref[z, head] = o[:, lanes].astype(o_ref.dtype)
                    lse_ref[z, head] = jnp.broadcast_to(lse[:, lanes], (8, TILE))


def attend(info, table, queries, state, sources, moves, chunks, wide, last, cost):
    vmem = pltpu.VMEM
    f32, bf16 = jnp.float32, jnp.bfloat16
    first = state is None
    keys = wide * TILE
    whole = pl.BlockSpec(memory_space=vmem)
    smem = pl.BlockSpec(memory_space=pltpu.SMEM)
    held = [jax.ShapeDtypeStruct((8, 2 * HD, 512), bf16), jax.ShapeDtypeStruct((8, HD, 512), f32),
            jax.ShapeDtypeStruct((8, 8, 512), f32), jax.ShapeDtypeStruct((8, 8, 512), f32)]
    o = jax.ShapeDtypeStruct((8, 2, HD, TILE), bf16)
    lse = jax.ShapeDtypeStruct((8, 2, 8, TILE), f32)
    before = list(queries) if first else list(state)
    return pl.pallas_call(
        functools.partial(attend_kernel, chunks, wide, first, last, moves),
        out_shape=[o, o, lse, lse] if last else held if first else held[1:],
        in_specs=[smem, smem] + [whole] * len(before)
        + [pl.BlockSpec(memory_space=pl.ANY)] * len(sources),
        out_specs=[whole] * (4 if first or last else 3),
        scratch_shapes=[vmem(h.shape, h.dtype) for h in held[1:] if last] + [
            vmem((chunks, wide, TILE, 2 * HD), bf16),
            vmem((keys, 512), f32),
            vmem((keys, 512), bf16),
            vmem((8, 512), f32),
            vmem((8, 512), f32),
            pltpu.SMEM((8 * chunks + 8,), jnp.int32),
            pltpu.SMEM((8 * chunks + 8,), jnp.int32),
            pltpu.SemaphoreType.DMA((sum(len(m) for m in moves),)),
        ],
        compiler_params=pltpu.CompilerParams(vmem_limit_bytes=30 * 2**20),
        cost_estimate=pl.CostEstimate(flops=int(cost * 1e9), bytes_accessed=8 * 2**20, transcendentals=0),
    )(info, table, *before, *sources)


def places(lengths):
    z, y, core = lax.axis_index("z"), lax.axis_index("y"), lax.axis_index("c")
    x = lax.axis_index("xh") * 2 + lax.axis_index("xl")

    def within(x, y):
        return (x // 2) * 2048 + y * 512 + (x % 2) * 256

    place = within(x, y)
    ends = jnp.cumsum(lengths) * BLOCK
    b = jnp.arange(4, dtype=jnp.int32)
    own_first = jnp.where(b < 2, core, 1 - core) * 128 + (b % 2) * 64
    offsets = jnp.concatenate([own_first, jnp.array([0, 192], jnp.int32)])
    tokens = jnp.arange(8, dtype=jnp.int32)[:, None] * PLANE + place + offsets[None, :]
    starts = jnp.max(jnp.where(ends[None, None, :] <= tokens[:, :, None], ends[None, None, :], 0), axis=2)
    info = jnp.concatenate([jnp.stack([place, core, core, core]), starts.reshape(48)]).astype(jnp.int32)

    shift = jnp.array(SHIFTS, jnp.int32)
    slots = jnp.array(SLOTS, jnp.int32)

    def blocks(group, near):
        plane = (z - slots[group] + 8) % 8
        near = jnp.array(near, jnp.int32)
        if group == 0:
            spot = within((x + shift + 4)[None, :] % 4, (y + near + 4)[:, None] % 4)
        else:
            spot = within((x + near + 4)[:, None] % 4, (y + shift + 4)[None, :] % 4)
        return (plane[:, None] * PLANE + spot.reshape(1, -1) + core * TILE).astype(jnp.int32)

    tables = []
    for near in ((0,), (-1, 1), (2,)):
        base = jnp.concatenate([blocks(0, near), blocks(1, near)], axis=0)
        tables.append(jnp.concatenate([base.reshape(-1), jnp.min(base, axis=1), jnp.max(base, axis=1) + (TILE - 1)]))
    return info, tables


def ring(n, d):
    return [(i, (i + d) % n) for i in range(n)]


def shards(queries, keys, values, lengths):
    swap = [(0, 1), (1, 0)]
    info, tables = places(lengths)
    odd = lax.axis_index("z") % 2
    k = keys.reshape(TILE, 2, HD).transpose(1, 0, 2)
    vt = values.reshape(TILE, 2, HD).transpose(1, 2, 0)
    kv = jnp.concatenate([k, vt], axis=2)
    mine = lax.dynamic_index_in_dim(kv, odd, 0, keepdims=True)
    theirs = lax.dynamic_index_in_dim(kv, 1 - odd, 0, keepdims=True)
    halves = []
    for group in SLOTS:
        halves.append(jnp.concatenate(
            [mine if d == 0 else lax.ppermute(theirs if d % 2 else mine, "z", ring(8, d)) for d in group], axis=0))

    qt = queries.reshape(TILE, 2, 4, 2, HD).transpose(2, 1, 3, 4, 0).reshape(8, 2, HD, TILE)
    q_own = lax.all_to_all(qt, "z", split_axis=0, concat_axis=0, tiled=True)
    q_other = lax.ppermute(q_own, "c", swap)

    def shift(value, axis, d):
        return lax.ppermute(value, axis, ring(4, d))

    def spread(value, axis):
        up, down = shift(value, axis, 1), shift(value, axis, -1)
        half = value.shape[0] // 2
        return up, down, shift(up[:half], axis, 1), shift(down[half:], axis, -1)

    xs, ys = ("xh", "xl"), "y"
    part_a = jnp.concatenate([halves[0], *spread(halves[0], xs)], axis=0)
    part_b = jnp.concatenate([halves[1], *spread(halves[1], ys)], axis=0)
    a_up, a_down, a_left, a_right = spread(part_a, ys)
    b_up, b_down, b_left, b_right = spread(part_b, xs)

    def laid(value):
        return value.reshape(-1, 4, TILE, 2 * HD)

    def moves(group, first, count, at=0):
        return [(j, (slice(group * 4, group * 4 + 4), first + j)) for j in range(at, at + count)]

    qq, *state = attend(info, tables[0], (q_own, q_other), None, [laid(part_a), laid(part_b)],
                   [moves(0, 0, 4), moves(1, 0, 4)], 8, 4, False, 4)
    state = attend(info, tables[1], None, [qq, *state], [laid(v) for v in (a_up, a_down, b_up, b_down)],
                   [moves(0, 0, 4), moves(0, 4, 4), moves(1, 0, 4), moves(1, 4, 4)], 8, 8, False, 8)
    o_own, o_other, lse_own, lse_other = attend(
        info, tables[2], None, [qq, *state], [laid(v) for v in (a_left, a_right, b_left, b_right)],
        [moves(0, 0, 2), moves(0, 2, 2), moves(1, 0, 2), moves(1, 2, 2)], 8, 4, True, 4)

    o_got = lax.ppermute(o_other, "c", swap)
    lse_got = lax.ppermute(lse_other, "c", swap)
    a, b = lse_own[:, :, :1], lse_got[:, :, :1]
    most = jnp.maximum(a, b)
    wa, wb = jnp.exp2(a - most), jnp.exp2(b - most)
    o = (o_own.astype(jnp.float32) * wa + o_got.astype(jnp.float32) * wb) / (wa + wb)
    back = lax.all_to_all(o.astype(jnp.bfloat16), "z", split_axis=0, concat_axis=0, tiled=True)
    return back.reshape(4, 2, 2, HD, TILE).transpose(4, 1, 0, 2, 3).reshape(TILE, 16 * HD)


def solution(mesh):
    fine = Mesh(mesh.devices.reshape(SIZES), AXES)
    spec = P(AXES, None)
    return jax.shard_map(
        shards, mesh=fine, in_specs=(spec, spec, spec, P()), out_specs=spec, check_vma=False
    )
```

```python
import functools
import math

import jax
import jax.numpy as jnp
from jax import lax
from jax.experimental import pallas as pl
from jax.experimental.pallas import tpu as pltpu
from jax.sharding import Mesh, PartitionSpec as P

HD = 128
BLOCK = 64
AXES = ("z", "xh", "y", "xl", "c")
SIZES = (8, 2, 4, 2, 2)
PLANE = 4096
TILE = 128
MASKED = -2e30
FLOOR = -1e29
LOG2E_SCALE = math.log2(math.e) / math.sqrt(HD)
SHIFTS = (0, -1, 1, 2)
PLAIN = 8
MIXED = 4
NOWHERE = 1 << 30


def layout(blocks):
    plain, mixed = blocks, 8 * (blocks // MIXED + 3)
    offsets = [2, 2 + plain]
    offsets.append(offsets[-1] + plain * PLAIN)
    offsets.append(offsets[-1] + mixed)
    offsets.append(offsets[-1] + mixed * MIXED)
    return offsets


def plan_kernel(parts, lengths, spot, info, *refs):
    tables, lists, ends = refs[:len(parts)], refs[len(parts):-1], refs[-1]
    x, y, core = spot[0], spot[1], spot[2]

    def within(x, y):
        return (x // 2) * 2048 + y * 512 + (x % 2) * 256

    place = within(x, y)
    info[0] = place
    info[1] = core

    def add_up(k, end):
        end = end + lengths[k] * BLOCK
        ends[k + 1] = end
        return end

    ends[0] = jnp.int32(0)
    lax.fori_loop(0, 16, add_up, jnp.int32(0))

    def query_plane(z, k):
        at = 4 + z * 6
        for b in range(4):
            token = z * PLANE + place + b * BLOCK
            k = lax.while_loop(lambda k: ends[k + 1] <= token, lambda k: k + 1, k)
            start = ends[k]
            info[at + jnp.where(core == b // 2, 0, 2) + b % 2] = start
            if b == 0:
                info[at + 4] = start
            if b == 3:
                info[at + 5] = start
        return k

    lax.fori_loop(0, 8, query_plane, jnp.int32(0))

    for (far, blocks), table, out in zip(parts, tables, lists):
        wide = blocks // 8
        plain_z, plain_b, mixed_z, mixed_b, _ = layout(blocks)
        for half in range(2):
            for n in range(wide):
                d, e = far[n // 4], SHIFTS[n % 4]
                dx, dy = (e, d) if half == 0 else (d, e)
                first = within((x + dx + 4) % 4, (y + dy + 4) % 4) + core * TILE
                for p in range(4):
                    table[half * 4 * wide + n * 4 + p] = first + (half * 4 + p) * PLANE
        table[blocks] = jnp.int32(NOWHERE)

        def plane(z, counts, table=table, out=out, wide=wide, plain_z=plain_z, plain_b=plain_b, mixed_z=mixed_z,
                  mixed_b=mixed_b, blocks=blocks):
            plain, mixed = counts
            begin = z * PLANE + place
            low, high = info[4 + z * 6 + 4], info[4 + z * 6 + 5]

            def key_plane(zk, found):
                b = (zk // 4) * (4 * wide) + zk % 4

                def sort_out(n, found):
                    p, m = found
                    base = table[b + n * 4]
                    need = (base + (TILE - 1) >= low) & (base <= begin + 255)
                    clear = (base + (TILE - 1) <= begin) & (base >= high)
                    out[plain_b + plain * PLAIN + p] = b + n * 4
                    out[mixed_b + mixed * MIXED + m] = b + n * 4
                    return p + jnp.where(need & clear, 1, 0), m + jnp.where(need & ~clear, 1, 0)

                for n in range(wide):
                    found = sort_out(n, found)
                return found

            p, m = lax.fori_loop(low // PLANE, z + 1, key_plane, (jnp.int32(0), jnp.int32(0)))
            full = p // PLAIN

            def left_over(i, m):
                out[mixed_b + mixed * MIXED + m] = out[plain_b + plain * PLAIN + i]
                return m + 1

            m = lax.fori_loop(full * PLAIN, p, left_over, m)
            some = (m + MIXED - 1) // MIXED

            def pad(i, carry):
                out[mixed_b + mixed * MIXED + i] = jnp.int32(blocks)
                return carry

            lax.fori_loop(m, some * MIXED, pad, 0)

            def name_plain(i, carry):
                out[plain_z + plain + i] = z
                return carry

            lax.fori_loop(0, full, name_plain, 0)

            def name_mixed(i, carry):
                out[mixed_z + mixed + i] = z
                return carry

            lax.fori_loop(0, some, name_mixed, 0)
            return plain + full, mixed + some

        plain, mixed = lax.fori_loop(0, 8, plane, (jnp.int32(0), jnp.int32(0)))
        out[0] = plain
        out[1] = mixed


def plan(lengths):
    spot = jnp.stack([lax.axis_index("xh") * 2 + lax.axis_index("xl"), lax.axis_index("y"), lax.axis_index("c")])
    smem = pl.BlockSpec(memory_space=pltpu.SMEM)
    parts = [((0,), 32), ((-1, 1), 64), ((2,), 32)]
    sizes = [52] + [b + 1 for _, b in parts] + [layout(b)[-1] + 8 for _, b in parts]
    info, *rest = pl.pallas_call(
        functools.partial(plan_kernel, parts),
        out_shape=[jax.ShapeDtypeStruct((n,), jnp.int32) for n in sizes],
        in_specs=[smem] * 2,
        out_specs=[smem] * len(sizes),
        scratch_shapes=[pltpu.SMEM((17,), jnp.int32)],
    )(lengths, spot.astype(jnp.int32))
    return info, rest[:3], rest[3:]


def pack_kernel(count, *refs):
    for half in range(2):
        at = 0
        for source in refs[half * count:(half + 1) * count]:
            refs[2 * count + half][at:at + source.shape[0]] = source[...]
            at += source.shape[0]


def pack(*halves):
    count = len(halves[0])
    whole = pl.BlockSpec(memory_space=pltpu.VMEM)
    out = [jax.ShapeDtypeStruct((sum(p.shape[0] for p in half),) + half[0].shape[1:], half[0].dtype) for half in halves]
    return pl.pallas_call(
        functools.partial(pack_kernel, count),
        out_shape=out,
        in_specs=[whole] * (2 * count),
        out_specs=[whole] * 2,
        compiler_params=pltpu.CompilerParams(vmem_limit_bytes=12 * 2**20),
    )(*halves[0], *halves[1])


def attend_kernel(blocks, first, last, moves, *refs):
    info, table, lists = refs[:3]
    rest = list(refs[3:])
    if first:
        q_own, q_other = rest[:2]
        del rest[:2]
    else:
        state = rest[:4]
        del rest[:4]
    sources = rest[:len(moves)]
    del rest[:len(moves)]
    if first:
        qq = rest.pop(0)
    else:
        qq = state[0]
    if last:
        o_own, o_other, lse_own, lse_other = rest[:4]
        del rest[:4]
    acc, peak, total, kv, score, weight, top, fade, sems = rest
    plain_z, plain_b, mixed_z, mixed_b, _ = layout(blocks)

    copies = [pltpu.make_async_copy(src, kv.at[pl.ds(at, size)], sems.at[i])
              for i, (src, (at, size)) in enumerate(zip(sources, moves))]
    for copy in copies:
        copy.start()
    kv[blocks] = jnp.zeros((TILE, 2 * HD), jnp.bfloat16)
    place = info[0]
    core = info[1]
    if first:
        for half, ref in enumerate((q_own, q_other)):
            for head in range(2):
                full = ref[:, head].astype(jnp.float32) * LOG2E_SCALE
                high = full.astype(jnp.bfloat16)
                lanes = slice(head * 256 + half * 128, head * 256 + half * 128 + 128)
                qq[:, :HD, lanes] = high
                qq[:, HD:, lanes] = (full - high.astype(jnp.float32)).astype(jnp.bfloat16)
        acc[...] = jnp.zeros_like(acc)
        total[...] = jnp.zeros_like(total)
        peak[...] = jnp.full_like(peak, FLOOR)
    else:
        for ref, old in zip((acc, peak, total), state[1:]):
            ref[...] = old[...]
    for copy in copies:
        copy.wait()

    def bounds(z):
        lane = lax.broadcasted_iota(jnp.int32, (1, 512), 1) % 256
        b = lane // 64
        at = 4 + z * 6
        start = jnp.where(b == 0, info[at], jnp.where(b == 1, info[at + 1],
                          jnp.where(b == 2, info[at + 2], info[at + 3])))
        part = jnp.where(lane < 128, core, 1 - core) * 128
        return start, z * PLANE + place + part + lane % 128

    def run(masked):
        wide = MIXED if masked else PLAIN
        keys = wide * TILE
        count = lists[1 if masked else 0]
        named, listed = (mixed_z, mixed_b) if masked else (plain_z, plain_b)

        def block(i, g):
            return lists[listed + i * wide + g]

        def scores_of(i):
            z = lists[named + i]
            k = jnp.concatenate([kv[block(i, g), :, :HD] for g in range(wide)], axis=0)
            s = jnp.dot(jnp.concatenate([k, k], axis=1), qq[z], preferred_element_type=jnp.float32)
            if masked:
                start, stop = bounds(z)
                row = lax.broadcasted_iota(jnp.int32, (TILE, 512), 0)
                parts = []
                for g in range(wide):
                    base = table[block(i, g)]
                    keep = (row >= start - base) & (row <= stop - base)
                    parts.append(jnp.where(keep, s[g * TILE:(g + 1) * TILE], MASKED))
                s = jnp.concatenate(parts, axis=0)
            score[:keys, :] = s
            top[...] = jnp.max(s.reshape(keys // 8, 8, 512), axis=0)

        def weigh(i):
            z = lists[named + i]
            old = peak[z]
            new = jnp.maximum(old, jnp.max(top[...], axis=0, keepdims=True))
            factor = jnp.exp2(old - new)
            fade[...] = factor
            peak[z] = new
            sums = total[z] * factor
            for u in range(keys // 16):
                rows = slice(u * 16, u * 16 + 16)
                p = jnp.exp2(score[rows, :].reshape(2, 8, 512) - new)
                sums = sums + (p[0] + p[1])
                weight[rows, :] = p.reshape(16, 512).astype(jnp.bfloat16)
            total[z] = sums

        def collect(i):
            z = lists[named + i]
            v = jnp.concatenate([kv[block(i, g), :, HD:] for g in range(wide)], axis=1)
            pv = jnp.dot(v, weight[:keys, :], preferred_element_type=jnp.float32)
            acc[z] = (acc[z].reshape(16, 8, 512) * fade[...] + pv.reshape(16, 8, 512)).reshape(HD, 512)

        @pl.when(count > 0)
        def _():
            scores_of(0)
            weight[:keys, :] = jnp.zeros((keys, 512), jnp.bfloat16)
            fade[...] = jnp.ones_like(fade)

            def body(i, carry):
                collect(jnp.maximum(i - 1, 0))
                weigh(i)
                scores_of(jnp.minimum(i + 1, count - 1))
                return carry

            lax.fori_loop(0, count, body, 0)
            collect(count - 1)

    run(True)
    run(False)
    if last:
        for z in range(8):
            l = jnp.sum(total[z], axis=0, keepdims=True)
            o = acc[z] / jnp.where(l > 0, l, 1.0)
            lse = jnp.where(l > 0, peak[z, :1] + jnp.log2(jnp.where(l > 0, l, 1.0)), FLOOR)
            for head in range(2):
                for half, (o_ref, lse_ref) in enumerate(((o_own, lse_own), (o_other, lse_other))):
                    lanes = slice(head * 256 + half * 128, head * 256 + half * 128 + 128)
                    o_ref[z, head] = o[:, lanes].astype(o_ref.dtype)
                    lse_ref[z, head] = jnp.broadcast_to(lse[:, lanes], (8, TILE))


def attend(info, table, lists, queries, state, sources, last, cost):
    vmem = pltpu.VMEM
    f32, bf16 = jnp.float32, jnp.bfloat16
    first = state is None
    sizes = [s.shape[0] for s in sources]
    blocks = sum(sizes)
    moves = [(sum(sizes[:i]), size) for i, size in enumerate(sizes)]
    keys = PLAIN * TILE
    whole = pl.BlockSpec(memory_space=vmem)
    smem = pl.BlockSpec(memory_space=pltpu.SMEM)
    held = [jax.ShapeDtypeStruct((8, 2 * HD, 512), bf16), jax.ShapeDtypeStruct((8, HD, 512), f32),
            jax.ShapeDtypeStruct((8, 8, 512), f32), jax.ShapeDtypeStruct((8, 8, 512), f32)]
    o = jax.ShapeDtypeStruct((8, 2, HD, TILE), bf16)
    lse = jax.ShapeDtypeStruct((8, 2, 8, TILE), f32)
    before = list(queries) if first else list(state)
    return pl.pallas_call(
        functools.partial(attend_kernel, blocks, first, last, moves),
        out_shape=[o, o, lse, lse] if last else held if first else held[1:],
        in_specs=[smem, smem, smem] + [whole] * len(before)
        + [pl.BlockSpec(memory_space=pl.ANY)] * len(sources),
        out_specs=[whole] * (4 if first or last else 3),
        scratch_shapes=[vmem(h.shape, h.dtype) for h in held[1:] if last] + [
            vmem((blocks + 1, TILE, 2 * HD), bf16),
            vmem((keys, 512), f32),
            vmem((keys, 512), bf16),
            vmem((8, 512), f32),
            vmem((8, 512), f32),
            pltpu.SemaphoreType.DMA((len(moves),)),
        ],
        compiler_params=pltpu.CompilerParams(vmem_limit_bytes=30 * 2**20),
        cost_estimate=pl.CostEstimate(flops=int(cost * 1e9), bytes_accessed=8 * 2**20, transcendentals=0),
    )(info, table, lists, *before, *sources)


def ring(n, d):
    return [(i, (i + d) % n) for i in range(n)]


def shards(queries, keys, values, lengths):
    swap = [(0, 1), (1, 0)]
    k = keys.reshape(TILE, 2, HD).transpose(1, 0, 2)
    vt = values.reshape(TILE, 2, HD).transpose(1, 2, 0)
    kv = jnp.concatenate([k, vt], axis=2)
    kv_send = jnp.concatenate([kv] * 4, axis=0)
    kv_z = lax.all_to_all(kv_send, "z", split_axis=0, concat_axis=0, tiled=True)
    qt = queries.reshape(TILE, 2, 4, 2, HD).transpose(2, 1, 3, 4, 0).reshape(8, 2, HD, TILE)
    planned = plan(lengths)
    qt, kv_z, planned = lax.optimization_barrier((qt, kv_z, planned))
    info, tables, lists = planned
    q_own = lax.all_to_all(qt, "z", split_axis=0, concat_axis=0, tiled=True)
    q_other = lax.ppermute(q_own, "c", swap)

    def shift(value, axis, d):
        return lax.ppermute(value, axis, ring(4, d))

    xs, ys = ("xh", "xl"), "y"
    first, second = kv_z[:4], kv_z[4:]
    near_a = [first] + [shift(first, xs, -d) for d in SHIFTS[1:]]
    near_b = [second] + [shift(second, ys, -d) for d in SHIFTS[1:]]
    part_a, part_b = pack(near_a, near_b)
    a_up, a_down = shift(part_a, ys, 1), shift(part_a, ys, -1)
    b_up, b_down = shift(part_b, xs, 1), shift(part_b, xs, -1)
    qq, *state = attend(info, tables[0], lists[0], (q_own, q_other), None, [part_a, part_b], False, 4)
    a_up, b_down, qq, state = lax.optimization_barrier((a_up, b_down, qq, state))
    a_far, b_far = shift(a_up, ys, 1), shift(b_down, xs, -1)
    state = attend(info, tables[1], lists[1], None, [qq, *state], [a_up, a_down, b_up, b_down], False, 8)
    o_own, o_other, lse_own, lse_other = attend(
        info, tables[2], lists[2], None, [qq, *state], [a_far, b_far], True, 4)

    o_got = lax.ppermute(o_other, "c", swap)
    lse_got = lax.ppermute(lse_other, "c", swap)
    a, b = lse_own[:, :, :1], lse_got[:, :, :1]
    most = jnp.maximum(a, b)
    wa, wb = jnp.exp2(a - most), jnp.exp2(b - most)
    o = (o_own.astype(jnp.float32) * wa + o_got.astype(jnp.float32) * wb) / (wa + wb)
    back = lax.all_to_all(o.astype(jnp.bfloat16), "z", split_axis=0, concat_axis=0, tiled=True)
    return back.reshape(4, 2, 2, HD, TILE).transpose(4, 1, 0, 2, 3).reshape(TILE, 16 * HD)


def solution(mesh):
    fine = Mesh(mesh.devices.reshape(SIZES), AXES)
    spec = P(AXES, None)
    return jax.shard_map(
        shards, mesh=fine, in_specs=(spec, spec, spec, P()), out_specs=spec, check_vma=False
    )
```

```python
import functools
import math

import jax
import jax.numpy as jnp
from jax import lax
from jax.experimental import pallas as pl
from jax.experimental.pallas import tpu as pltpu
from jax.sharding import Mesh, PartitionSpec as P

HD = 128
BLOCK = 64
AXES = ("z", "xh", "y", "xl", "c")
SIZES = (8, 2, 4, 2, 2)
PLANE = 4096
TILE = 128
MASKED = -2e30
FLOOR = -1e29
LOG2E_SCALE = math.log2(math.e) / math.sqrt(HD)
SHIFTS = (0, -1, 1, 2)
UNITS = ((8, False), (4, False), (2, False), (1, False), (4, True), (1, True))
WIDEST = UNITS[0][0]


def layout(blocks):
    offsets = [len(UNITS) + 2]
    for wide, masked in UNITS:
        most = 24 if wide == 1 and masked else blocks if wide == 8 else 2 * blocks if masked else 8
        offsets.append(offsets[-1] + most)
    return offsets[:-1] + [offsets[-1], offsets[-1] + 8 * blocks, offsets[-1] + 16 * blocks + 8]


def plan_kernel(parts, lengths, spot, info, *refs):
    tables, lists, ends = refs[:len(parts)], refs[len(parts):-1], refs[-1]
    x, y, core = spot[0], spot[1], spot[2]

    def within(x, y):
        return (x // 2) * 2048 + y * 512 + (x % 2) * 256

    place = within(x, y)
    info[0] = place
    info[1] = core

    def add_up(k, end):
        end = end + lengths[k] * BLOCK
        ends[k + 1] = end
        return end

    ends[0] = jnp.int32(0)
    lax.fori_loop(0, 16, add_up, jnp.int32(0))

    def query_plane(z, k):
        at = 4 + z * 6
        for b in range(4):
            token = z * PLANE + place + b * BLOCK
            k = lax.while_loop(lambda k: ends[k + 1] <= token, lambda k: k + 1, k)
            start = ends[k]
            info[at + jnp.where(core == b // 2, 0, 2) + b % 2] = start
            if b == 0:
                info[at + 4] = start
            if b == 3:
                info[at + 5] = start
        return k

    lax.fori_loop(0, 8, query_plane, jnp.int32(0))

    for (far, blocks), table, out in zip(parts, tables, lists):
        wide = blocks // 8
        *kinds, plain_b, mixed_b, _ = layout(blocks)
        for half in range(2):
            for n in range(wide):
                d, e = far[n // 4], SHIFTS[n % 4]
                dx, dy = (e, d) if half == 0 else (d, e)
                first = within((x + dx + 4) % 4, (y + dy + 4) % 4) + core * TILE
                for p in range(4):
                    table[half * 4 * wide + n * 4 + p] = first + (half * 4 + p) * PLANE

        def plane(z, counts, table=table, out=out, wide=wide, kinds=kinds, plain_b=plain_b, mixed_b=mixed_b):
            plain, mixed, *counts = counts
            begin = z * PLANE + place
            low, high = info[4 + z * 6 + 4], info[4 + z * 6 + 5]

            def key_plane(zk, found):
                p, m = found
                b = (zk // 4) * (4 * wide) + zk % 4
                for n in range(wide):
                    base = table[b + n * 4]
                    need = (base + (TILE - 1) >= low) & (base <= begin + 255)
                    clear = (base + (TILE - 1) <= begin) & (base >= high)
                    out[p] = b + n * 4
                    out[m] = b + n * 4
                    p, m = p + jnp.where(need & clear, 1, 0), m + jnp.where(need & ~clear, 1, 0)
                return p, m

            p, m = lax.fori_loop(low // PLANE, z + 1, key_plane, (plain_b + plain, mixed_b + mixed))
            plain_at, mixed_at = plain_b + plain, mixed_b + mixed
            left, more = p - plain_at, m - mixed_at
            for kind, (size, masked) in enumerate(UNITS):
                at, count = (mixed_at, more) if masked else (plain_at, left)
                n = count // size

                def name(i, carry, kind=kind, size=size, at=at, first=counts[kind]):
                    out[kinds[kind] + first + i] = (at + i * size) * 8 + z
                    return carry

                lax.fori_loop(0, n, name, 0)
                counts[kind] = counts[kind] + n
                if masked:
                    mixed_at, more = at + n * size, count - n * size
                else:
                    plain_at, left = at + n * size, count - n * size
            return (p - plain_b, m - mixed_b, *counts)

        none = (jnp.int32(0),) * (2 + len(UNITS))
        counts = lax.fori_loop(0, 8, plane, none)[2:]
        for kind, count in enumerate(counts):
            out[kind] = count


def plan(lengths):
    spot = jnp.stack([lax.axis_index("xh") * 2 + lax.axis_index("xl"), lax.axis_index("y"), lax.axis_index("c")])
    smem = pl.BlockSpec(memory_space=pltpu.SMEM)
    parts = [((0,), 32), ((-1, 1), 64), ((2,), 32)]
    sizes = [52] + [b for _, b in parts] + [layout(b)[-1] for _, b in parts]
    info, *rest = pl.pallas_call(
        functools.partial(plan_kernel, parts),
        out_shape=[jax.ShapeDtypeStruct((n,), jnp.int32) for n in sizes],
        in_specs=[smem] * 2,
        out_specs=[smem] * len(sizes),
        scratch_shapes=[pltpu.SMEM((17,), jnp.int32)],
    )(lengths, spot.astype(jnp.int32))
    return info, rest[:3], rest[3:]


def pack_kernel(count, *refs):
    for half in range(2):
        at = 0
        for source in refs[half * count:(half + 1) * count]:
            refs[2 * count + half][at:at + source.shape[0]] = source[...]
            at += source.shape[0]


def pack(*halves):
    count = len(halves[0])
    whole = pl.BlockSpec(memory_space=pltpu.VMEM)
    out = [jax.ShapeDtypeStruct((sum(p.shape[0] for p in half),) + half[0].shape[1:], half[0].dtype) for half in halves]
    return pl.pallas_call(
        functools.partial(pack_kernel, count),
        out_shape=out,
        in_specs=[whole] * (2 * count),
        out_specs=[whole] * 2,
        compiler_params=pltpu.CompilerParams(vmem_limit_bytes=12 * 2**20),
    )(*halves[0], *halves[1])


def attend_kernel(blocks, first, last, moves, *refs):
    info, table, lists = refs[:3]
    rest = list(refs[3:])
    if first:
        q_own, q_other = rest[:2]
        del rest[:2]
    else:
        state = rest[:4]
        del rest[:4]
    sources = rest[:len(moves)]
    del rest[:len(moves)]
    if first:
        qq = rest.pop(0)
    else:
        qq = state[0]
    if last:
        o_own, o_other, lse_own, lse_other = rest[:4]
        del rest[:4]
    acc, peak, total, kv, score, weight, top, fade, sems = rest
    kinds = layout(blocks)

    copies = [pltpu.make_async_copy(src, kv.at[pl.ds(at, size)], sems.at[i])
              for i, (src, (at, size)) in enumerate(zip(sources, moves))]
    for copy in copies:
        copy.start()
    place = info[0]
    core = info[1]
    if first:
        for half, ref in enumerate((q_own, q_other)):
            for head in range(2):
                full = ref[:, head].astype(jnp.float32) * LOG2E_SCALE
                high = full.astype(jnp.bfloat16)
                lanes = slice(head * 256 + half * 128, head * 256 + half * 128 + 128)
                qq[:, :HD, lanes] = high
                qq[:, HD:, lanes] = (full - high.astype(jnp.float32)).astype(jnp.bfloat16)
        acc[...] = jnp.zeros_like(acc)
        total[...] = jnp.zeros_like(total)
        peak[...] = jnp.full_like(peak, FLOOR)
    else:
        for ref, old in zip((acc, peak, total), state[1:]):
            ref[...] = old[...]
    for copy in copies:
        copy.wait()

    def bounds(z):
        lane = lax.broadcasted_iota(jnp.int32, (1, 512), 1) % 256
        b = lane // 64
        at = 4 + z * 6
        start = jnp.where(b == 0, info[at], jnp.where(b == 1, info[at + 1],
                          jnp.where(b == 2, info[at + 2], info[at + 3])))
        part = jnp.where(lane < 128, core, 1 - core) * 128
        return start, z * PLANE + place + part + lane % 128

    def run(kind):
        wide, masked = UNITS[kind]
        keys = wide * TILE
        count = lists[kind]

        def plane_of(i):
            return lists[kinds[kind] + i] % 8

        def block(i, g):
            return lists[lists[kinds[kind] + i] // 8 + g]

        def scores_of(i):
            z = plane_of(i)
            k = jnp.concatenate([kv[block(i, g), :, :HD] for g in range(wide)], axis=0)
            s = jnp.dot(jnp.concatenate([k, k], axis=1), qq[z], preferred_element_type=jnp.float32)
            if masked:
                start, stop = bounds(z)
                row = lax.broadcasted_iota(jnp.int32, (TILE, 512), 0)
                parts = []
                for g in range(wide):
                    base = table[block(i, g)]
                    keep = (row >= start - base) & (row <= stop - base)
                    parts.append(jnp.where(keep, s[g * TILE:(g + 1) * TILE], MASKED))
                s = jnp.concatenate(parts, axis=0)
            score[:keys, :] = s
            top[...] = jnp.max(s.reshape(keys // 8, 8, 512), axis=0)

        def weigh(i):
            z = plane_of(i)
            old = peak[z]
            new = jnp.maximum(old, jnp.max(top[...], axis=0, keepdims=True))
            factor = jnp.exp2(old - new)
            fade[...] = factor
            peak[z] = new
            sums = total[z] * factor
            for u in range(keys // 16):
                rows = slice(u * 16, u * 16 + 16)
                p = jnp.exp2(score[rows, :].reshape(2, 8, 512) - new)
                sums = sums + (p[0] + p[1])
                weight[rows, :] = p.reshape(16, 512).astype(jnp.bfloat16)
            total[z] = sums

        def collect(i):
            z = plane_of(i)
            v = jnp.concatenate([kv[block(i, g), :, HD:] for g in range(wide)], axis=1)
            pv = jnp.dot(v, weight[:keys, :], preferred_element_type=jnp.float32)
            acc[z] = (acc[z].reshape(16, 8, 512) * fade[...] + pv.reshape(16, 8, 512)).reshape(HD, 512)

        @pl.when(count > 0)
        def _():
            scores_of(0)
            weight[:keys, :] = jnp.zeros((keys, 512), jnp.bfloat16)
            fade[...] = jnp.ones_like(fade)

            def body(i, carry):
                collect(jnp.maximum(i - 1, 0))
                weigh(i)
                scores_of(jnp.minimum(i + 1, count - 1))
                return carry

            lax.fori_loop(0, count, body, 0)
            collect(count - 1)

    for kind in range(len(UNITS)):
        run(kind)
    if last:
        for z in range(8):
            l = jnp.sum(total[z], axis=0, keepdims=True)
            o = acc[z] / jnp.where(l > 0, l, 1.0)
            lse = jnp.where(l > 0, peak[z, :1] + jnp.log2(jnp.where(l > 0, l, 1.0)), FLOOR)
            for head in range(2):
                for half, (o_ref, lse_ref) in enumerate(((o_own, lse_own), (o_other, lse_other))):
                    lanes = slice(head * 256 + half * 128, head * 256 + half * 128 + 128)
                    o_ref[z, head] = o[:, lanes].astype(o_ref.dtype)
                    lse_ref[z, head] = jnp.broadcast_to(lse[:, lanes], (8, TILE))


def attend(info, table, lists, queries, state, sources, last, cost):
    vmem = pltpu.VMEM
    f32, bf16 = jnp.float32, jnp.bfloat16
    first = state is None
    sizes = [s.shape[0] for s in sources]
    blocks = sum(sizes)
    moves = [(sum(sizes[:i]), size) for i, size in enumerate(sizes)]
    keys = WIDEST * TILE
    whole = pl.BlockSpec(memory_space=vmem)
    smem = pl.BlockSpec(memory_space=pltpu.SMEM)
    held = [jax.ShapeDtypeStruct((8, 2 * HD, 512), bf16), jax.ShapeDtypeStruct((8, HD, 512), f32),
            jax.ShapeDtypeStruct((8, 8, 512), f32), jax.ShapeDtypeStruct((8, 8, 512), f32)]
    o = jax.ShapeDtypeStruct((8, 2, HD, TILE), bf16)
    lse = jax.ShapeDtypeStruct((8, 2, 8, TILE), f32)
    before = list(queries) if first else list(state)
    return pl.pallas_call(
        functools.partial(attend_kernel, blocks, first, last, moves),
        out_shape=[o, o, lse, lse] if last else held if first else held[1:],
        in_specs=[smem, smem, smem] + [whole] * len(before)
        + [pl.BlockSpec(memory_space=pl.ANY)] * len(sources),
        out_specs=[whole] * (4 if first or last else 3),
        scratch_shapes=[vmem(h.shape, h.dtype) for h in held[1:] if last] + [
            vmem((blocks, TILE, 2 * HD), bf16),
            vmem((keys, 512), f32),
            vmem((keys, 512), bf16),
            vmem((8, 512), f32),
            vmem((8, 512), f32),
            pltpu.SemaphoreType.DMA((len(moves),)),
        ],
        compiler_params=pltpu.CompilerParams(vmem_limit_bytes=30 * 2**20),
        cost_estimate=pl.CostEstimate(flops=int(cost * 1e9), bytes_accessed=8 * 2**20, transcendentals=0),
    )(info, table, lists, *before, *sources)


def ring(n, d):
    return [(i, (i + d) % n) for i in range(n)]


def shards(queries, keys, values, lengths):
    swap = [(0, 1), (1, 0)]
    k = keys.reshape(TILE, 2, HD).transpose(1, 0, 2)
    vt = values.reshape(TILE, 2, HD).transpose(1, 2, 0)
    kv = jnp.concatenate([k, vt], axis=2)
    kv_send = jnp.concatenate([kv] * 4, axis=0)
    kv_z = lax.all_to_all(kv_send, "z", split_axis=0, concat_axis=0, tiled=True)
    qt = queries.reshape(TILE, 2, 4, 2, HD).transpose(2, 1, 3, 4, 0).reshape(8, 2, HD, TILE)
    planned = plan(lengths)
    qt, kv_z, planned = lax.optimization_barrier((qt, kv_z, planned))
    info, tables, lists = planned
    q_own = lax.all_to_all(qt, "z", split_axis=0, concat_axis=0, tiled=True)
    q_other = lax.ppermute(q_own, "c", swap)

    def shift(value, axis, d):
        return lax.ppermute(value, axis, ring(4, d))

    xs, ys = ("xh", "xl"), "y"
    first, second = kv_z[:4], kv_z[4:]
    near_a = [first] + [shift(first, xs, -d) for d in SHIFTS[1:]]
    near_b = [second] + [shift(second, ys, -d) for d in SHIFTS[1:]]
    part_a, part_b = pack(near_a, near_b)
    a_up, a_down = shift(part_a, ys, 1), shift(part_a, ys, -1)
    b_up, b_down = shift(part_b, xs, 1), shift(part_b, xs, -1)
    qq, *state = attend(info, tables[0], lists[0], (q_own, q_other), None, [part_a, part_b], False, 4)
    a_up, b_down, qq, state = lax.optimization_barrier((a_up, b_down, qq, state))
    a_far, b_far = shift(a_up, ys, 1), shift(b_down, xs, -1)
    state = attend(info, tables[1], lists[1], None, [qq, *state], [a_up, a_down, b_up, b_down], False, 8)
    o_own, o_other, lse_own, lse_other = attend(
        info, tables[2], lists[2], None, [qq, *state], [a_far, b_far], True, 4)

    o_got = lax.ppermute(o_other, "c", swap)
    lse_got = lax.ppermute(lse_other, "c", swap)
    a, b = lse_own[:, :, :1], lse_got[:, :, :1]
    most = jnp.maximum(a, b)
    wa, wb = jnp.exp2(a - most), jnp.exp2(b - most)
    o = (o_own.astype(jnp.float32) * wa + o_got.astype(jnp.float32) * wb) / (wa + wb)
    back = lax.all_to_all(o.astype(jnp.bfloat16), "z", split_axis=0, concat_axis=0, tiled=True)
    return back.reshape(4, 2, 2, HD, TILE).transpose(4, 1, 0, 2, 3).reshape(TILE, 16 * HD)


def solution(mesh):
    fine = Mesh(mesh.devices.reshape(SIZES), AXES)
    spec = P(AXES, None)
    return jax.shard_map(
        shards, mesh=fine, in_specs=(spec, spec, spec, P()), out_specs=spec, check_vma=False
    )
```

```python
import functools
import math

import jax
import jax.numpy as jnp
from jax import lax
from jax.experimental import pallas as pl
from jax.experimental.pallas import tpu as pltpu
from jax.sharding import Mesh, PartitionSpec as P

HD = 128
BLOCK = 64
AXES = ("z", "xh", "y", "xl", "c")
SIZES = (8, 2, 4, 2, 2)
PLANE = 4096
TILE = 128
MASKED = -2e30
FLOOR = -1e29
NEVER = 1e30
LOG2E_SCALE = math.log2(math.e) / math.sqrt(HD)
SHIFTS = (0, -1, 1, 2)
UNITS = ((8, False), (4, False), (2, False), (1, False), (1, True))
WIDEST = UNITS[0][0]


def layout(blocks):
    offsets = [len(UNITS) + 2]
    for wide, masked in UNITS:
        most = blocks if wide == 8 else 8 * 3 if masked else 8
        offsets.append(offsets[-1] + most)
    return offsets[:-1] + [offsets[-1], offsets[-1] + 8 * blocks, offsets[-1] + 16 * blocks + 8]


def plan_kernel(parts, lengths, spot, info, *refs):
    tables, lists, ends = refs[:len(parts)], refs[len(parts):-1], refs[-1]
    x, y, core = spot[0], spot[1], spot[2]

    def within(x, y):
        return (x // 2) * 2048 + y * 512 + (x % 2) * 256

    place = within(x, y)
    info[0] = place
    info[1] = core

    def add_up(k, end):
        end = end + lengths[k] * BLOCK
        ends[k + 1] = end
        return end

    ends[0] = jnp.int32(0)
    lax.fori_loop(0, 16, add_up, jnp.int32(0))

    def query_plane(z, k):
        at = 4 + z * 6
        for b in range(4):
            token = z * PLANE + place + b * BLOCK
            k = lax.while_loop(lambda k: ends[k + 1] <= token, lambda k: k + 1, k)
            start = ends[k]
            info[at + jnp.where(core == b // 2, 0, 2) + b % 2] = start
            if b == 0:
                info[at + 4] = start
            if b == 3:
                info[at + 5] = start
        return k

    lax.fori_loop(0, 8, query_plane, jnp.int32(0))

    for (far, blocks), table, out in zip(parts, tables, lists):
        wide = blocks // 8
        *kinds, plain_b, mixed_b, _ = layout(blocks)
        for half in range(2):
            for n in range(wide):
                d, e = far[n // 4], SHIFTS[n % 4]
                dx, dy = (e, d) if half == 0 else (d, e)
                first = within((x + dx + 4) % 4, (y + dy + 4) % 4) + core * TILE
                for p in range(4):
                    table[half * 4 * wide + n * 4 + p] = first + (half * 4 + p) * PLANE

        def plane(z, counts, table=table, out=out, wide=wide, kinds=kinds, plain_b=plain_b, mixed_b=mixed_b):
            plain, mixed, *counts = counts
            begin = z * PLANE + place
            low = info[4 + z * 6 + 4]

            def key_plane(zk, found):
                p, m = found
                b = (zk // 4) * (4 * wide) + zk % 4
                for n in range(wide):
                    base = table[b + n * 4]
                    need = (base + (TILE - 1) >= low) & (base <= begin + 255)
                    clear = (base + (TILE - 1) < begin) & (base >= low)
                    out[p] = b + n * 4
                    out[m] = b + n * 4
                    p, m = p + jnp.where(need & clear, 1, 0), m + jnp.where(need & ~clear, 1, 0)
                return p, m

            p, m = lax.fori_loop(low // PLANE, z + 1, key_plane, (plain_b + plain, mixed_b + mixed))
            plain_at, mixed_at = plain_b + plain, mixed_b + mixed
            left, more = p - plain_at, m - mixed_at
            for kind, (size, masked) in enumerate(UNITS):
                at, count = (mixed_at, more) if masked else (plain_at, left)
                n = count // size

                def name(i, carry, kind=kind, size=size, at=at, first=counts[kind]):
                    out[kinds[kind] + first + i] = (at + i * size) * 8 + z
                    return carry

                lax.fori_loop(0, n, name, 0)
                counts[kind] = counts[kind] + n
                if masked:
                    mixed_at, more = at + n * size, count - n * size
                else:
                    plain_at, left = at + n * size, count - n * size
            return (p - plain_b, m - mixed_b, *counts)

        none = (jnp.int32(0),) * (2 + len(UNITS))
        counts = lax.fori_loop(0, 8, plane, none)[2:]
        for kind, count in enumerate(counts):
            out[kind] = count


def plan(lengths):
    spot = jnp.stack([lax.axis_index("xh") * 2 + lax.axis_index("xl"), lax.axis_index("y"), lax.axis_index("c")])
    smem = pl.BlockSpec(memory_space=pltpu.SMEM)
    parts = [((0,), 32), ((-1, 1), 64), ((2,), 32)]
    sizes = [52] + [b for _, b in parts] + [layout(b)[-1] for _, b in parts]
    info, *rest = pl.pallas_call(
        functools.partial(plan_kernel, parts),
        out_shape=[jax.ShapeDtypeStruct((n,), jnp.int32) for n in sizes],
        in_specs=[smem] * 2,
        out_specs=[smem] * len(sizes),
        scratch_shapes=[pltpu.SMEM((17,), jnp.int32)],
    )(lengths, spot.astype(jnp.int32))
    return info, rest[:3], rest[3:]


def prepare_kernel(keys, values, out):
    for head in range(2):
        lanes = slice(head * HD, head * HD + HD)
        k = keys[:, lanes]
        vt = values[:, lanes].astype(jnp.float32).T.astype(jnp.bfloat16)
        for z in range(head, 8, 2):
            out[z, :, :HD] = k
            out[z, :, HD:] = vt


def prepare(keys, values):
    whole = pl.BlockSpec(memory_space=pltpu.VMEM)
    return pl.pallas_call(
        prepare_kernel,
        out_shape=jax.ShapeDtypeStruct((8, TILE, 2 * HD), jnp.bfloat16),
        in_specs=[whole] * 2,
        out_specs=whole,
    )(keys, values)


def pack_kernel(count, *refs):
    for half in range(2):
        at = 0
        for source in refs[half * count:(half + 1) * count]:
            refs[2 * count + half][at:at + source.shape[0]] = source[...]
            at += source.shape[0]


def pack(*halves):
    count = len(halves[0])
    whole = pl.BlockSpec(memory_space=pltpu.VMEM)
    out = [jax.ShapeDtypeStruct((sum(p.shape[0] for p in half),) + half[0].shape[1:], half[0].dtype) for half in halves]
    return pl.pallas_call(
        functools.partial(pack_kernel, count),
        out_shape=out,
        in_specs=[whole] * (2 * count),
        out_specs=[whole] * 2,
        compiler_params=pltpu.CompilerParams(vmem_limit_bytes=12 * 2**20),
    )(*halves[0], *halves[1])


def attend_kernel(blocks, first, last, moves, *refs):
    info, table, lists = refs[:3]
    rest = list(refs[3:])
    if first:
        q_own, q_other = rest[:2]
        del rest[:2]
    else:
        state = rest[:4]
        del rest[:4]
    sources = rest[:len(moves)]
    del rest[:len(moves)]
    if first:
        qq = rest.pop(0)
    else:
        qq = state[0]
    if last:
        o_own, o_other, lse_own, lse_other = rest[:4]
        del rest[:4]
    acc, peak, total, kv, score, weight, top, fade, off, sems = rest
    kinds = layout(blocks)

    copies = [pltpu.make_async_copy(src, kv.at[pl.ds(at, size)], sems.at[i])
              for i, (src, (at, size)) in enumerate(zip(sources, moves))]
    for copy in copies:
        copy.start()
    place = info[0]
    core = info[1]
    if first:
        for half, ref in enumerate((q_own, q_other)):
            for head in range(2):
                full = ref[:, head].astype(jnp.float32) * LOG2E_SCALE
                high = full.astype(jnp.bfloat16)
                lanes = slice(head * 256 + half * 128, head * 256 + half * 128 + 128)
                qq[:, :HD, lanes] = high
                qq[:, HD:, lanes] = (full - high.astype(jnp.float32)).astype(jnp.bfloat16)
        acc[...] = jnp.zeros_like(acc)
        total[...] = jnp.zeros_like(total)
        peak[...] = jnp.full_like(peak, FLOOR)
    else:
        for ref, old in zip((acc, peak, total), state[1:]):
            ref[...] = old[...]
    for copy in copies:
        copy.wait()

    def bounds(z):
        lane = lax.broadcasted_iota(jnp.int32, (1, 512), 1) % 256
        b = lane // 64
        at = 4 + z * 6
        start = jnp.where(b == 0, info[at], jnp.where(b == 1, info[at + 1],
                          jnp.where(b == 2, info[at + 2], info[at + 3])))
        part = jnp.where(lane < 128, core, 1 - core) * 128
        return start, z * PLANE + place + part + lane % 128

    for z in range(8):
        late = bounds(z)[0] > z * PLANE + place
        off[z] = jnp.broadcast_to(jnp.where(late, NEVER, 0.0), (8, 512))

    def run(kind):
        wide, masked = UNITS[kind]
        keys = wide * TILE
        count = lists[kind]

        def plane_of(i):
            return lists[kinds[kind] + i] % 8

        def block(i, g):
            return lists[lists[kinds[kind] + i] // 8 + g]

        def scores_of(i):
            z = plane_of(i)
            k = jnp.concatenate([kv[block(i, g), :, :HD] for g in range(wide)], axis=0)
            s = jnp.dot(jnp.concatenate([k, k], axis=1), qq[z], preferred_element_type=jnp.float32)
            if masked:
                start, stop = bounds(z)
                row = lax.broadcasted_iota(jnp.int32, (TILE, 512), 0)
                parts = []
                for g in range(wide):
                    base = table[block(i, g)]
                    keep = (row >= start - base) & (row <= stop - base)
                    parts.append(jnp.where(keep, s[g * TILE:(g + 1) * TILE], MASKED))
                s = jnp.concatenate(parts, axis=0)
            score[:keys, :] = s
            top[...] = jnp.max(s.reshape(keys // 8, 8, 512), axis=0)

        def weigh(i):
            z = plane_of(i)
            old = peak[z]
            most = jnp.max(top[...], axis=0, keepdims=True)
            new = jnp.maximum(old, most if masked else most - off[z])
            factor = jnp.exp2(old - new)
            fade[...] = factor
            peak[z] = new
            if not masked:
                new = new + off[z]
            sums = total[z] * factor
            for u in range(keys // 16):
                rows = slice(u * 16, u * 16 + 16)
                p = jnp.exp2(score[rows, :].reshape(2, 8, 512) - new)
                sums = sums + (p[0] + p[1])
                weight[rows, :] = p.reshape(16, 512).astype(jnp.bfloat16)
            total[z] = sums

        def collect(i):
            z = plane_of(i)
            v = jnp.concatenate([kv[block(i, g), :, HD:] for g in range(wide)], axis=1)
            pv = jnp.dot(v, weight[:keys, :], preferred_element_type=jnp.float32)
            acc[z] = (acc[z].reshape(16, 8, 512) * fade[...] + pv.reshape(16, 8, 512)).reshape(HD, 512)

        @pl.when(count > 0)
        def _():
            scores_of(0)
            weight[:keys, :] = jnp.zeros((keys, 512), jnp.bfloat16)
            fade[...] = jnp.ones_like(fade)

            def body(i, carry):
                collect(jnp.maximum(i - 1, 0))
                weigh(i)
                scores_of(jnp.minimum(i + 1, count - 1))
                return carry

            lax.fori_loop(0, count, body, 0)
            collect(count - 1)

    for kind in range(len(UNITS)):
        run(kind)
    if last:
        for z in range(8):
            l = jnp.sum(total[z], axis=0, keepdims=True)
            o = acc[z] / jnp.where(l > 0, l, 1.0)
            lse = jnp.where(l > 0, peak[z, :1] + jnp.log2(jnp.where(l > 0, l, 1.0)), FLOOR)
            for head in range(2):
                for half, (o_ref, lse_ref) in enumerate(((o_own, lse_own), (o_other, lse_other))):
                    lanes = slice(head * 256 + half * 128, head * 256 + half * 128 + 128)
                    o_ref[z, head] = o[:, lanes].astype(o_ref.dtype)
                    lse_ref[z, head] = jnp.broadcast_to(lse[:, lanes], (8, TILE))


def attend(info, table, lists, queries, state, sources, last, cost):
    vmem = pltpu.VMEM
    f32, bf16 = jnp.float32, jnp.bfloat16
    first = state is None
    sizes = [s.shape[0] for s in sources]
    blocks = sum(sizes)
    moves = [(sum(sizes[:i]), size) for i, size in enumerate(sizes)]
    keys = WIDEST * TILE
    whole = pl.BlockSpec(memory_space=vmem)
    smem = pl.BlockSpec(memory_space=pltpu.SMEM)
    held = [jax.ShapeDtypeStruct((8, 2 * HD, 512), bf16), jax.ShapeDtypeStruct((8, HD, 512), f32),
            jax.ShapeDtypeStruct((8, 8, 512), f32), jax.ShapeDtypeStruct((8, 8, 512), f32)]
    o = jax.ShapeDtypeStruct((8, 2, HD, TILE), bf16)
    lse = jax.ShapeDtypeStruct((8, 2, 8, TILE), f32)
    before = list(queries) if first else list(state)
    return pl.pallas_call(
        functools.partial(attend_kernel, blocks, first, last, moves),
        out_shape=[o, o, lse, lse] if last else held if first else held[1:],
        in_specs=[smem, smem, smem] + [whole] * len(before)
        + [pl.BlockSpec(memory_space=pl.ANY)] * len(sources),
        out_specs=[whole] * (4 if first or last else 3),
        scratch_shapes=[vmem(h.shape, h.dtype) for h in held[1:] if last] + [
            vmem((blocks, TILE, 2 * HD), bf16),
            vmem((keys, 512), f32),
            vmem((keys, 512), bf16),
            vmem((8, 512), f32),
            vmem((8, 512), f32),
            vmem((8, 8, 512), f32),
            pltpu.SemaphoreType.DMA((len(moves),)),
        ],
        compiler_params=pltpu.CompilerParams(vmem_limit_bytes=30 * 2**20),
        cost_estimate=pl.CostEstimate(flops=int(cost * 1e9), bytes_accessed=8 * 2**20, transcendentals=0),
    )(info, table, lists, *before, *sources)


def ring(n, d):
    return [(i, (i + d) % n) for i in range(n)]


def shards(queries, keys, values, lengths):
    swap = [(0, 1), (1, 0)]
    kv_send = prepare(keys, values)
    kv_z = lax.all_to_all(kv_send, "z", split_axis=0, concat_axis=0, tiled=True)
    qt = queries.reshape(TILE, 2, 4, 2, HD).transpose(2, 1, 3, 4, 0).reshape(8, 2, HD, TILE)
    planned = plan(lengths)
    qt, kv_z, planned = lax.optimization_barrier((qt, kv_z, planned))
    info, tables, lists = planned
    q_own = lax.all_to_all(qt, "z", split_axis=0, concat_axis=0, tiled=True)
    q_other = lax.ppermute(q_own, "c", swap)

    def shift(value, axis, d):
        return lax.ppermute(value, axis, ring(4, d))

    xs, ys = ("xh", "xl"), "y"
    first, second = kv_z[:4], kv_z[4:]
    near_a = [first] + [shift(first, xs, -d) for d in SHIFTS[1:]]
    near_b = [second] + [shift(second, ys, -d) for d in SHIFTS[1:]]
    part_a, part_b = pack(near_a, near_b)
    a_up, a_down = shift(part_a, ys, 1), shift(part_a, ys, -1)
    b_up, b_down = shift(part_b, xs, 1), shift(part_b, xs, -1)
    qq, *state = attend(info, tables[0], lists[0], (q_own, q_other), None, [part_a, part_b], False, 4)
    a_up, b_down, qq, state = lax.optimization_barrier((a_up, b_down, qq, state))
    a_far, b_far = shift(a_up, ys, 1), shift(b_down, xs, -1)
    state = attend(info, tables[1], lists[1], None, [qq, *state], [a_up, a_down, b_up, b_down], False, 8)
    o_own, o_other, lse_own, lse_other = attend(
        info, tables[2], lists[2], None, [qq, *state], [a_far, b_far], True, 4)

    o_got = lax.ppermute(o_other, "c", swap)
    lse_got = lax.ppermute(lse_other, "c", swap)
    a, b = lse_own[:, :, :1], lse_got[:, :, :1]
    most = jnp.maximum(a, b)
    wa, wb = jnp.exp2(a - most), jnp.exp2(b - most)
    o = (o_own.astype(jnp.float32) * wa + o_got.astype(jnp.float32) * wb) / (wa + wb)
    back = lax.all_to_all(o.astype(jnp.bfloat16), "z", split_axis=0, concat_axis=0, tiled=True)
    return back.reshape(4, 2, 2, HD, TILE).transpose(4, 1, 0, 2, 3).reshape(TILE, 16 * HD)


def solution(mesh):
    fine = Mesh(mesh.devices.reshape(SIZES), AXES)
    spec = P(AXES, None)
    return jax.shard_map(
        shards, mesh=fine, in_specs=(spec, spec, spec, P()), out_specs=spec, check_vma=False
    )
```

```python
import functools
import math

import jax
import jax.numpy as jnp
from jax import lax
from jax.experimental import pallas as pl
from jax.experimental.pallas import tpu as pltpu
from jax.sharding import Mesh, PartitionSpec as P

HD = 128
BLOCK = 64
AXES = ("z", "xh", "y", "xl", "c")
SIZES = (8, 2, 4, 2, 2)
PLANE = 4096
TILE = 128
MASKED = -2e30
FLOOR = -1e29
NEVER = 1e30
LOG2E_SCALE = math.log2(math.e) / math.sqrt(HD)
SHIFTS = (0, -1, 1, 2)
UNITS = ((8, False), (4, False), (2, False), (1, True))
WIDEST = UNITS[0][0]


def layout(blocks):
    offsets = [len(UNITS) + 2]
    for wide, masked in UNITS:
        most = blocks if wide == 8 else 8 * 4 if masked else 8
        offsets.append(offsets[-1] + most)
    return offsets[:-1] + [offsets[-1], offsets[-1] + 8 * blocks, offsets[-1] + 16 * blocks + 8]


def plan_kernel(parts, lengths, spot, info, *refs):
    tables, lists, ends = refs[:len(parts)], refs[len(parts):-1], refs[-1]
    x, y, core = spot[0], spot[1], spot[2]

    def within(x, y):
        return (x // 2) * 2048 + y * 512 + (x % 2) * 256

    place = within(x, y)
    info[0] = place
    info[1] = core

    def add_up(k, end):
        end = end + lengths[k] * BLOCK
        ends[k + 1] = end
        return end

    ends[0] = jnp.int32(0)
    lax.fori_loop(0, 16, add_up, jnp.int32(0))

    def query_plane(z, k):
        at = 4 + z * 6
        for b in range(4):
            token = z * PLANE + place + b * BLOCK
            k = lax.while_loop(lambda k: ends[k + 1] <= token, lambda k: k + 1, k)
            start = ends[k]
            info[at + jnp.where(core == b // 2, 0, 2) + b % 2] = start
            if b == 0:
                info[at + 4] = start
            if b == 3:
                info[at + 5] = start
        return k

    lax.fori_loop(0, 8, query_plane, jnp.int32(0))

    for (far, blocks), table, out in zip(parts, tables, lists):
        wide = blocks // 8
        *kinds, plain_b, mixed_b, _ = layout(blocks)
        for half in range(2):
            for n in range(wide):
                d, e = far[n // 4] * (1 - 2 * core), SHIFTS[n % 4]
                dx, dy = (e, d) if half == 0 else (d, e)
                first = within((x + dx + 4) % 4, (y + dy + 4) % 4) + core * TILE
                for p in range(4):
                    table[half * 4 * wide + n * 4 + p] = first + (half * 4 + p) * PLANE

        def plane(z, counts, table=table, out=out, wide=wide, kinds=kinds, plain_b=plain_b, mixed_b=mixed_b):
            plain, mixed, *counts = counts
            begin = z * PLANE + place
            low = info[4 + z * 6 + 4]

            def key_plane(zk, found):
                p, m = found
                b = (zk // 4) * (4 * wide) + zk % 4
                for n in range(wide):
                    base = table[b + n * 4]
                    need = (base + (TILE - 1) >= low) & (base <= begin + 255)
                    clear = (base + (TILE - 1) < begin) & (base >= low)
                    out[p] = b + n * 4
                    out[m] = b + n * 4
                    p, m = p + jnp.where(need & clear, 1, 0), m + jnp.where(need & ~clear, 1, 0)
                return p, m

            p, m = lax.fori_loop(low // PLANE, z + 1, key_plane, (plain_b + plain, mixed_b + mixed))
            plain_at, mixed_at = plain_b + plain, mixed_b + mixed
            left, more = p - plain_at, m - mixed_at
            for kind, (size, masked) in enumerate(UNITS):
                if masked:
                    out[mixed_at + more] = out[plain_at]
                    more = more + left
                at, count = (mixed_at, more) if masked else (plain_at, left)
                n = count // size

                def name(i, carry, kind=kind, size=size, at=at, first=counts[kind]):
                    out[kinds[kind] + first + i] = (at + i * size) * 8 + z
                    return carry

                lax.fori_loop(0, n, name, 0)
                counts[kind] = counts[kind] + n
                if masked:
                    mixed_at, more = at + n * size, count - n * size
                else:
                    plain_at, left = at + n * size, count - n * size
            return (p - plain_b, mixed_at - mixed_b, *counts)

        none = (jnp.int32(0),) * (2 + len(UNITS))
        counts = lax.fori_loop(0, 8, plane, none)[2:]
        for kind, count in enumerate(counts):
            out[kind] = count


def plan(lengths):
    spot = jnp.stack([lax.axis_index("xh") * 2 + lax.axis_index("xl"), lax.axis_index("y"), lax.axis_index("c")])
    smem = pl.BlockSpec(memory_space=pltpu.SMEM)
    parts = [((0,), 32), ((-1, 1), 64), ((2,), 32)]
    sizes = [52] + [b for _, b in parts] + [layout(b)[-1] for _, b in parts]
    info, *rest = pl.pallas_call(
        functools.partial(plan_kernel, parts),
        out_shape=[jax.ShapeDtypeStruct((n,), jnp.int32) for n in sizes],
        in_specs=[smem] * 2,
        out_specs=[smem] * len(sizes),
        scratch_shapes=[pltpu.SMEM((17,), jnp.int32)],
    )(lengths, spot.astype(jnp.int32))
    return info, rest[:3], rest[3:]


def prepare_kernel(keys, values, out):
    for head in range(2):
        lanes = slice(head * HD, head * HD + HD)
        k = keys[:, lanes]
        vt = values[:, lanes].astype(jnp.float32).T.astype(jnp.bfloat16)
        for z in range(head, 8, 2):
            out[z, :, :HD] = k
            out[z, :, HD:] = vt


def prepare(keys, values):
    whole = pl.BlockSpec(memory_space=pltpu.VMEM)
    return pl.pallas_call(
        prepare_kernel,
        out_shape=jax.ShapeDtypeStruct((8, TILE, 2 * HD), jnp.bfloat16),
        in_specs=[whole] * 2,
        out_specs=whole,
    )(keys, values)


def pack_kernel(count, *refs):
    for half in range(2):
        at = 0
        for source in refs[half * count:(half + 1) * count]:
            refs[2 * count + half][at:at + source.shape[0]] = source[...]
            at += source.shape[0]


def pack(*halves):
    count = len(halves[0])
    whole = pl.BlockSpec(memory_space=pltpu.VMEM)
    out = [jax.ShapeDtypeStruct((sum(p.shape[0] for p in half),) + half[0].shape[1:], half[0].dtype) for half in halves]
    return pl.pallas_call(
        functools.partial(pack_kernel, count),
        out_shape=out,
        in_specs=[whole] * (2 * count),
        out_specs=[whole] * 2,
        compiler_params=pltpu.CompilerParams(vmem_limit_bytes=12 * 2**20),
    )(*halves[0], *halves[1])


def attend_kernel(blocks, first, last, moves, *refs):
    info, table, lists = refs[:3]
    rest = list(refs[3:])
    if first:
        q_own, q_other = rest[:2]
        del rest[:2]
    else:
        state = rest[:4]
        del rest[:4]
    sources = rest[:len(moves)]
    del rest[:len(moves)]
    if first:
        qq = rest.pop(0)
    else:
        qq = state[0]
    if last:
        o_own, o_other, lse_own, lse_other = rest[:4]
        del rest[:4]
    acc, peak, total, kv, score, weight, top, fade, off, sems = rest
    kinds = layout(blocks)

    copies = [pltpu.make_async_copy(src, kv.at[pl.ds(at, size)], sems.at[i])
              for i, (src, (at, size)) in enumerate(zip(sources, moves))]
    for copy in copies:
        copy.start()
    place = info[0]
    core = info[1]
    if first:
        for half, ref in enumerate((q_own, q_other)):
            for head in range(2):
                full = ref[:, head].astype(jnp.float32) * LOG2E_SCALE
                high = full.astype(jnp.bfloat16)
                lanes = slice(head * 256 + half * 128, head * 256 + half * 128 + 128)
                qq[:, :HD, lanes] = high
                qq[:, HD:, lanes] = (full - high.astype(jnp.float32)).astype(jnp.bfloat16)
        acc[...] = jnp.zeros_like(acc)
        total[...] = jnp.zeros_like(total)
        peak[...] = jnp.full_like(peak, FLOOR)
    else:
        for ref, old in zip((acc, peak, total), state[1:]):
            ref[...] = old[...]
    for copy in copies:
        copy.wait()

    def bounds(z):
        lane = lax.broadcasted_iota(jnp.int32, (1, 512), 1) % 256
        b = lane // 64
        at = 4 + z * 6
        start = jnp.where(b == 0, info[at], jnp.where(b == 1, info[at + 1],
                          jnp.where(b == 2, info[at + 2], info[at + 3])))
        part = jnp.where(lane < 128, core, 1 - core) * 128
        return start, z * PLANE + place + part + lane % 128

    for z in range(8):
        late = bounds(z)[0] > z * PLANE + place
        off[z] = jnp.broadcast_to(jnp.where(late, NEVER, 0.0), (8, 512))

    def run(kind):
        wide, masked = UNITS[kind]
        keys = wide * TILE
        count = lists[kind]

        def plane_of(i):
            return lists[kinds[kind] + i] % 8

        def block(i, g):
            return lists[lists[kinds[kind] + i] // 8 + g]

        def scores_of(i):
            z = plane_of(i)
            k = jnp.concatenate([kv[block(i, g), :, :HD] for g in range(wide)], axis=0)
            s = jnp.dot(jnp.concatenate([k, k], axis=1), qq[z], preferred_element_type=jnp.float32)
            if masked:
                start, stop = bounds(z)
                row = lax.broadcasted_iota(jnp.int32, (TILE, 512), 0)
                parts = []
                for g in range(wide):
                    base = table[block(i, g)]
                    keep = (row >= start - base) & (row <= stop - base)
                    parts.append(jnp.where(keep, s[g * TILE:(g + 1) * TILE], MASKED))
                s = jnp.concatenate(parts, axis=0)
            score[:keys, :] = s
            top[...] = jnp.max(s.reshape(keys // 8, 8, 512), axis=0)

        def weigh(i):
            z = plane_of(i)
            old = peak[z]
            most = jnp.max(top[...], axis=0, keepdims=True)
            new = jnp.maximum(old, most if masked else most - off[z])
            factor = jnp.exp2(old - new)
            fade[...] = factor
            peak[z] = new
            if not masked:
                new = new + off[z]
            sums = total[z] * factor
            for u in range(keys // 16):
                rows = slice(u * 16, u * 16 + 16)
                p = jnp.exp2(score[rows, :].reshape(2, 8, 512) - new)
                sums = sums + (p[0] + p[1])
                weight[rows, :] = p.reshape(16, 512).astype(jnp.bfloat16)
            total[z] = sums

        def collect(i):
            z = plane_of(i)
            v = jnp.concatenate([kv[block(i, g), :, HD:] for g in range(wide)], axis=1)
            pv = jnp.dot(v, weight[:keys, :], preferred_element_type=jnp.float32)
            acc[z] = (acc[z].reshape(16, 8, 512) * fade[...] + pv.reshape(16, 8, 512)).reshape(HD, 512)

        @pl.when(count > 0)
        def _():
            scores_of(0)
            weight[:keys, :] = jnp.zeros((keys, 512), jnp.bfloat16)
            fade[...] = jnp.ones_like(fade)

            def body(i, carry):
                collect(jnp.maximum(i - 1, 0))
                weigh(i)
                scores_of(jnp.minimum(i + 1, count - 1))
                return carry

            lax.fori_loop(0, count, body, 0)
            collect(count - 1)

    for kind in range(len(UNITS)):
        run(kind)
    if last:
        for z in range(8):
            l = jnp.sum(total[z], axis=0, keepdims=True)
            o = acc[z] / jnp.where(l > 0, l, 1.0)
            lse = jnp.where(l > 0, peak[z, :1] + jnp.log2(jnp.where(l > 0, l, 1.0)), FLOOR)
            for head in range(2):
                for half, (o_ref, lse_ref) in enumerate(((o_own, lse_own), (o_other, lse_other))):
                    lanes = slice(head * 256 + half * 128, head * 256 + half * 128 + 128)
                    o_ref[z, head] = o[:, lanes].astype(o_ref.dtype)
                    lse_ref[z, head] = jnp.broadcast_to(lse[:, lanes], (8, TILE))


def attend(info, table, lists, queries, state, sources, last, cost):
    vmem = pltpu.VMEM
    f32, bf16 = jnp.float32, jnp.bfloat16
    first = state is None
    sizes = [s.shape[0] for s in sources]
    blocks = sum(sizes)
    moves = [(sum(sizes[:i]), size) for i, size in enumerate(sizes)]
    keys = WIDEST * TILE
    whole = pl.BlockSpec(memory_space=vmem)
    smem = pl.BlockSpec(memory_space=pltpu.SMEM)
    held = [jax.ShapeDtypeStruct((8, 2 * HD, 512), bf16), jax.ShapeDtypeStruct((8, HD, 512), f32),
            jax.ShapeDtypeStruct((8, 8, 512), f32), jax.ShapeDtypeStruct((8, 8, 512), f32)]
    o = jax.ShapeDtypeStruct((8, 2, HD, TILE), bf16)
    lse = jax.ShapeDtypeStruct((8, 2, 8, TILE), f32)
    before = list(queries) if first else list(state)
    return pl.pallas_call(
        functools.partial(attend_kernel, blocks, first, last, moves),
        out_shape=[o, o, lse, lse] if last else held if first else held[1:],
        in_specs=[smem, smem, smem] + [whole] * len(before)
        + [pl.BlockSpec(memory_space=pl.ANY)] * len(sources),
        out_specs=[whole] * (4 if first or last else 3),
        scratch_shapes=[vmem(h.shape, h.dtype) for h in held[1:] if last] + [
            vmem((blocks, TILE, 2 * HD), bf16),
            vmem((keys, 512), f32),
            vmem((keys, 512), bf16),
            vmem((8, 512), f32),
            vmem((8, 512), f32),
            vmem((8, 8, 512), f32),
            pltpu.SemaphoreType.DMA((len(moves),)),
        ],
        compiler_params=pltpu.CompilerParams(vmem_limit_bytes=30 * 2**20),
        cost_estimate=pl.CostEstimate(flops=int(cost * 1e9), bytes_accessed=8 * 2**20, transcendentals=0),
    )(info, table, lists, *before, *sources)


def ring(n, d):
    return [(i, (i + d) % n) for i in range(n)]


def shards(queries, keys, values, lengths):
    swap = [(0, 1), (1, 0)]
    kv_send = prepare(keys, values)
    kv_z = lax.all_to_all(kv_send, "z", split_axis=0, concat_axis=0, tiled=True)
    qt = queries.reshape(TILE, 2, 4, 2, HD).transpose(2, 1, 3, 4, 0).reshape(8, 2, HD, TILE)
    planned = plan(lengths)
    qt, kv_z, planned = lax.optimization_barrier((qt, kv_z, planned))
    info, tables, lists = planned
    q_own = lax.all_to_all(qt, "z", split_axis=0, concat_axis=0, tiled=True)
    q_other = lax.ppermute(q_own, "c", swap)

    def shift(value, axis, d):
        return lax.ppermute(value, axis, ring(4, d))

    xs, ys = ("xh", "xl"), "y"
    first, second = kv_z[:4], kv_z[4:]
    near_a, near_b = [first] + [None] * 3, [second] + [None] * 3
    for n in (3, 1, 2):
        near_a[n] = shift(first, xs, -SHIFTS[n])
        near_b[n] = shift(second, ys, -SHIFTS[n])
    part_a, part_b = pack(near_a, near_b)
    def turn(value, axes, d):
        pairs = [(2 * i + c, 2 * ((i + d - 2 * d * c) % 4) + c) for i in range(4) for c in range(2)]
        return lax.ppermute(value, (*axes, "c"), pairs)

    a_up, b_down = turn(part_a, ("y",), 1), turn(part_b, xs, -1)
    a_down, b_up = turn(part_a, ("y",), -1), turn(part_b, xs, 1)
    qq, *state = attend(info, tables[0], lists[0], (q_own, q_other), None, [part_a, part_b], False, 4)
    a_up, b_down, qq, state = lax.optimization_barrier((a_up, b_down, qq, state))
    a_far, b_far = turn(a_up, ("y",), 1), turn(b_down, xs, -1)
    state = attend(info, tables[1], lists[1], None, [qq, *state], [a_up, a_down, b_up, b_down], False, 8)
    o_own, o_other, lse_own, lse_other = attend(
        info, tables[2], lists[2], None, [qq, *state], [a_far, b_far], True, 4)

    o_got = lax.ppermute(o_other, "c", swap)
    lse_got = lax.ppermute(lse_other, "c", swap)
    a, b = lse_own[:, :, :1], lse_got[:, :, :1]
    most = jnp.maximum(a, b)
    wa, wb = jnp.exp2(a - most), jnp.exp2(b - most)
    o = (o_own.astype(jnp.float32) * wa + o_got.astype(jnp.float32) * wb) / (wa + wb)
    back = lax.all_to_all(o.astype(jnp.bfloat16), "z", split_axis=0, concat_axis=0, tiled=True)
    return back.reshape(4, 2, 2, HD, TILE).transpose(4, 1, 0, 2, 3).reshape(TILE, 16 * HD)


def solution(mesh):
    fine = Mesh(mesh.devices.reshape(SIZES), AXES)
    spec = P(AXES, None)
    return jax.shard_map(
        shards, mesh=fine, in_specs=(spec, spec, spec, P()), out_specs=spec, check_vma=False
    )
```

```python
import functools
import math

import jax
import jax.numpy as jnp
from jax import lax
from jax.experimental import pallas as pl
from jax.experimental.pallas import tpu as pltpu
from jax.sharding import Mesh, PartitionSpec as P

HD = 128
BLOCK = 64
AXES = ("z", "xh", "y", "xl", "c")
SIZES = (8, 2, 4, 2, 2)
PLANE = 4096
TILE = 128
MASKED = -2e30
FLOOR = -1e29
NEVER = 1e30
LOG2E_SCALE = math.log2(math.e) / math.sqrt(HD)
SHIFTS = (0, -1, 1, 2)
UNITS = ((8, False), (4, False), (2, False), (1, True))
WIDEST = UNITS[0][0]


def layout(blocks):
    offsets = [len(UNITS) + 2]
    for wide, masked in UNITS:
        most = blocks if wide == 8 else 8 * 4 if masked else 8
        offsets.append(offsets[-1] + most)
    return offsets[:-1] + [offsets[-1], offsets[-1] + 8 * blocks, offsets[-1] + 16 * blocks + 8]


def plan_kernel(parts, lengths, spot, info, *refs):
    tables, lists, ends = refs[:len(parts)], refs[len(parts):-1], refs[-1]
    x, y, core = spot[0], spot[1], spot[2]

    def within(x, y):
        return (x // 2) * 2048 + y * 512 + (x % 2) * 256

    place = within(x, y)
    info[0] = place
    info[1] = core

    def add_up(k, end):
        end = end + lengths[k] * BLOCK
        ends[k + 1] = end
        return end

    ends[0] = jnp.int32(0)
    lax.fori_loop(0, 16, add_up, jnp.int32(0))

    def query_plane(z, k):
        at = 4 + z * 6
        for b in range(4):
            token = z * PLANE + place + b * BLOCK
            k = lax.while_loop(lambda k: ends[k + 1] <= token, lambda k: k + 1, k)
            start = ends[k]
            info[at + jnp.where(core == b // 2, 0, 2) + b % 2] = start
            if b == 0:
                info[at + 4] = start
            if b == 3:
                info[at + 5] = start
        return k

    lax.fori_loop(0, 8, query_plane, jnp.int32(0))

    for (far, blocks), table, out in zip(parts, tables, lists):
        wide = blocks // 8
        *kinds, plain_b, mixed_b, _ = layout(blocks)
        for half in range(2):
            for n in range(wide):
                d, e = far[n // 4] * (1 - 2 * core), SHIFTS[n % 4]
                dx, dy = (e, d) if half == 0 else (d, e)
                first = within((x + dx + 4) % 4, (y + dy + 4) % 4) + core * TILE
                for p in range(4):
                    table[half * 4 * wide + n * 4 + p] = first + (half * 4 + p) * PLANE

        def plane(z, counts, table=table, out=out, wide=wide, kinds=kinds, plain_b=plain_b, mixed_b=mixed_b):
            plain, mixed, *counts = counts
            begin = z * PLANE + place
            low = info[4 + z * 6 + 4]

            def key_plane(zk, found):
                p, m = found
                b = (zk // 4) * (4 * wide) + zk % 4
                for n in range(wide):
                    base = table[b + n * 4]
                    need = (base + (TILE - 1) >= low) & (base <= begin + 255)
                    clear = (base + (TILE - 1) < begin) & (base >= low)
                    out[p] = b + n * 4
                    out[m] = b + n * 4
                    p, m = p + jnp.where(need & clear, 1, 0), m + jnp.where(need & ~clear, 1, 0)
                return p, m

            p, m = lax.fori_loop(low // PLANE, z + 1, key_plane, (plain_b + plain, mixed_b + mixed))
            plain_at, mixed_at = plain_b + plain, mixed_b + mixed
            left, more = p - plain_at, m - mixed_at
            for kind, (size, masked) in enumerate(UNITS):
                if masked:
                    out[mixed_at + more] = out[plain_at]
                    more = more + left
                at, count = (mixed_at, more) if masked else (plain_at, left)
                n = count // size

                def name(i, carry, kind=kind, size=size, at=at, first=counts[kind]):
                    out[kinds[kind] + first + i] = (at + i * size) * 8 + z
                    return carry

                lax.fori_loop(0, n, name, 0)
                counts[kind] = counts[kind] + n
                if masked:
                    mixed_at, more = at + n * size, count - n * size
                else:
                    plain_at, left = at + n * size, count - n * size
            return (p - plain_b, mixed_at - mixed_b, *counts)

        none = (jnp.int32(0),) * (2 + len(UNITS))
        counts = lax.fori_loop(0, 8, plane, none)[2:]
        for kind, count in enumerate(counts):
            out[kind] = count


def plan(lengths):
    spot = jnp.stack([lax.axis_index("xh") * 2 + lax.axis_index("xl"), lax.axis_index("y"), lax.axis_index("c")])
    smem = pl.BlockSpec(memory_space=pltpu.SMEM)
    parts = [((0,), 32), ((-1, 1), 64), ((2,), 32)]
    sizes = [52] + [b for _, b in parts] + [layout(b)[-1] for _, b in parts]
    info, *rest = pl.pallas_call(
        functools.partial(plan_kernel, parts),
        out_shape=[jax.ShapeDtypeStruct((n,), jnp.int32) for n in sizes],
        in_specs=[smem] * 2,
        out_specs=[smem] * len(sizes),
        scratch_shapes=[pltpu.SMEM((17,), jnp.int32)],
    )(lengths, spot.astype(jnp.int32))
    return info, rest[:3], rest[3:]


def prepare_kernel(keys, values, out):
    for head in range(2):
        lanes = slice(head * HD, head * HD + HD)
        k = keys[:, lanes]
        vt = values[:, lanes].astype(jnp.float32).T.astype(jnp.bfloat16)
        for z in range(head, 8, 2):
            out[z, :, :HD] = k
            out[z, :, HD:] = vt


def prepare(keys, values):
    whole = pl.BlockSpec(memory_space=pltpu.VMEM)
    return pl.pallas_call(
        prepare_kernel,
        out_shape=jax.ShapeDtypeStruct((8, TILE, 2 * HD), jnp.bfloat16),
        in_specs=[whole] * 2,
        out_specs=whole,
    )(keys, values)


def pack_kernel(count, *refs):
    for half in range(2):
        at = 0
        for source in refs[half * count:(half + 1) * count]:
            refs[2 * count + half][at:at + source.shape[0]] = source[...]
            at += source.shape[0]


def pack(*halves):
    count = len(halves[0])
    whole = pl.BlockSpec(memory_space=pltpu.VMEM)
    out = [jax.ShapeDtypeStruct((sum(p.shape[0] for p in half),) + half[0].shape[1:], half[0].dtype) for half in halves]
    return pl.pallas_call(
        functools.partial(pack_kernel, count),
        out_shape=out,
        in_specs=[whole] * (2 * count),
        out_specs=[whole] * 2,
        compiler_params=pltpu.CompilerParams(vmem_limit_bytes=12 * 2**20),
    )(*halves[0], *halves[1])


def attend_kernel(blocks, first, last, moves, *refs):
    info, table, lists = refs[:3]
    rest = list(refs[3:])
    if first:
        q_own, q_other = rest[:2]
        del rest[:2]
    else:
        state = rest[:4]
        del rest[:4]
    sources = rest[:len(moves)]
    del rest[:len(moves)]
    if first:
        qq = rest.pop(0)
    else:
        qq = state[0]
    if last:
        o_own, o_other, lse_own, lse_other = rest[:4]
        del rest[:4]
    acc, peak, total, kv, score, weight, top, fade, off, sems = rest
    kinds = layout(blocks)

    copies = [pltpu.make_async_copy(src, kv.at[pl.ds(at, size)], sems.at[i])
              for i, (src, (at, size)) in enumerate(zip(sources, moves))]
    for copy in copies:
        copy.start()
    place = info[0]
    core = info[1]
    if first:
        for half, ref in enumerate((q_own, q_other)):
            for head in range(2):
                full = ref[:, head].astype(jnp.float32) * LOG2E_SCALE
                high = full.astype(jnp.bfloat16)
                lanes = slice(head * 256 + half * 128, head * 256 + half * 128 + 128)
                qq[:, :HD, lanes] = high
                qq[:, HD:, lanes] = (full - high.astype(jnp.float32)).astype(jnp.bfloat16)
        acc[...] = jnp.zeros_like(acc)
        total[...] = jnp.zeros_like(total)
        peak[...] = jnp.full_like(peak, FLOOR)
    else:
        for ref, old in zip((acc, peak, total), state[1:]):
            ref[...] = old[...]
    for copy in copies:
        copy.wait()

    def bounds(z):
        lane = lax.broadcasted_iota(jnp.int32, (1, 512), 1) % 256
        b = lane // 64
        at = 4 + z * 6
        start = jnp.where(b == 0, info[at], jnp.where(b == 1, info[at + 1],
                          jnp.where(b == 2, info[at + 2], info[at + 3])))
        part = jnp.where(lane < 128, core, 1 - core) * 128
        return start, z * PLANE + place + part + lane % 128

    for z in range(8):
        late = bounds(z)[0] > z * PLANE + place
        off[z] = jnp.broadcast_to(jnp.where(late, NEVER, 0.0), (8, 512))

    def run(kind):
        wide, masked = UNITS[kind]
        keys = wide * TILE
        count = lists[kind]

        def plane_of(i):
            return lists[kinds[kind] + i] % 8

        def block(i, g):
            return lists[lists[kinds[kind] + i] // 8 + g]

        def scores_of(i):
            z = plane_of(i)
            k = jnp.concatenate([kv[block(i, g), :, :HD] for g in range(wide)], axis=0)
            s = jnp.dot(jnp.concatenate([k, k], axis=1), qq[z], preferred_element_type=jnp.float32)
            if masked:
                start, stop = bounds(z)
                row = lax.broadcasted_iota(jnp.int32, (TILE, 512), 0)
                parts = []
                for g in range(wide):
                    base = table[block(i, g)]
                    keep = (row >= start - base) & (row <= stop - base)
                    parts.append(jnp.where(keep, s[g * TILE:(g + 1) * TILE], MASKED))
                s = jnp.concatenate(parts, axis=0)
            score[:keys, :] = s
            top[...] = jnp.max(s.reshape(keys // 8, 8, 512), axis=0)

        def weigh(i):
            z = plane_of(i)
            old = peak[z]
            most = jnp.max(top[...], axis=0, keepdims=True)
            new = jnp.maximum(old, most if masked else most - off[z])
            factor = jnp.exp2(old - new)
            fade[...] = factor
            peak[z] = new
            if not masked:
                new = new + off[z]
            sums = total[z] * factor
            for u in range(keys // 16):
                rows = slice(u * 16, u * 16 + 16)
                p = jnp.exp2(score[rows, :].reshape(2, 8, 512) - new)
                sums = sums + (p[0] + p[1])
                weight[rows, :] = p.reshape(16, 512).astype(jnp.bfloat16)
            total[z] = sums

        def collect(i):
            z = plane_of(i)
            v = jnp.concatenate([kv[block(i, g), :, HD:] for g in range(wide)], axis=1)
            pv = jnp.dot(v, weight[:keys, :], preferred_element_type=jnp.float32)
            acc[z] = (acc[z].reshape(16, 8, 512) * fade[...] + pv.reshape(16, 8, 512)).reshape(HD, 512)

        @pl.when(count > 0)
        def _():
            scores_of(0)
            weight[:keys, :] = jnp.zeros((keys, 512), jnp.bfloat16)
            fade[...] = jnp.ones_like(fade)

            def body(i, carry):
                collect(jnp.maximum(i - 1, 0))
                weigh(i)
                scores_of(jnp.minimum(i + 1, count - 1))
                return carry

            lax.fori_loop(0, count, body, 0)
            collect(count - 1)

    for kind in range(len(UNITS)):
        run(kind)
    if last:
        for z in range(8):
            l = jnp.sum(total[z], axis=0, keepdims=True)
            o = acc[z] / jnp.where(l > 0, l, 1.0)
            lse = jnp.where(l > 0, peak[z, :1] + jnp.log2(jnp.where(l > 0, l, 1.0)), FLOOR)
            for head in range(2):
                for half, (o_ref, lse_ref) in enumerate(((o_own, lse_own), (o_other, lse_other))):
                    lanes = slice(head * 256 + half * 128, head * 256 + half * 128 + 128)
                    o_ref[z, head] = o[:, lanes].astype(o_ref.dtype)
                    lse_ref[2 * z + head:2 * z + head + 1, :] = lse[:, lanes]


def attend(info, table, lists, queries, state, sources, last, cost):
    vmem = pltpu.VMEM
    f32, bf16 = jnp.float32, jnp.bfloat16
    first = state is None
    sizes = [s.shape[0] for s in sources]
    blocks = sum(sizes)
    moves = [(sum(sizes[:i]), size) for i, size in enumerate(sizes)]
    keys = WIDEST * TILE
    whole = pl.BlockSpec(memory_space=vmem)
    smem = pl.BlockSpec(memory_space=pltpu.SMEM)
    held = [jax.ShapeDtypeStruct((8, 2 * HD, 512), bf16), jax.ShapeDtypeStruct((8, HD, 512), f32),
            jax.ShapeDtypeStruct((8, 8, 512), f32), jax.ShapeDtypeStruct((8, 8, 512), f32)]
    o = jax.ShapeDtypeStruct((8, 2, HD, TILE), bf16)
    lse = jax.ShapeDtypeStruct((16, TILE), f32)
    before = list(queries) if first else list(state)
    return pl.pallas_call(
        functools.partial(attend_kernel, blocks, first, last, moves),
        out_shape=[o, o, lse, lse] if last else held if first else held[1:],
        in_specs=[smem, smem, smem] + [whole] * len(before)
        + [pl.BlockSpec(memory_space=pl.ANY)] * len(sources),
        out_specs=[whole] * (4 if first or last else 3),
        scratch_shapes=[vmem(h.shape, h.dtype) for h in held[1:] if last] + [
            vmem((blocks, TILE, 2 * HD), bf16),
            vmem((keys, 512), f32),
            vmem((keys, 512), bf16),
            vmem((8, 512), f32),
            vmem((8, 512), f32),
            vmem((8, 8, 512), f32),
            pltpu.SemaphoreType.DMA((len(moves),)),
        ],
        compiler_params=pltpu.CompilerParams(vmem_limit_bytes=30 * 2**20),
        cost_estimate=pl.CostEstimate(flops=int(cost * 1e9), bytes_accessed=8 * 2**20, transcendentals=0),
    )(info, table, lists, *before, *sources)


def ring(n, d):
    return [(i, (i + d) % n) for i in range(n)]


def shards(queries, keys, values, lengths):
    swap = [(0, 1), (1, 0)]
    kv_send = prepare(keys, values)
    kv_z = lax.all_to_all(kv_send, "z", split_axis=0, concat_axis=0, tiled=True)
    qt = queries.reshape(TILE, 2, 4, 2, HD).transpose(2, 1, 3, 4, 0).reshape(8, 2, HD, TILE)
    planned = plan(lengths)
    qt, kv_z, planned = lax.optimization_barrier((qt, kv_z, planned))
    info, tables, lists = planned
    q_own = lax.all_to_all(qt, "z", split_axis=0, concat_axis=0, tiled=True)
    q_other = lax.ppermute(q_own, "c", swap)

    def shift(value, axis, d):
        return lax.ppermute(value, axis, ring(4, d))

    xs, ys = ("xh", "xl"), "y"
    first, second = kv_z[:4], kv_z[4:]
    near_a, near_b = [first] + [None] * 3, [second] + [None] * 3
    for n in (3, 1, 2):
        near_a[n] = shift(first, xs, -SHIFTS[n])
        near_b[n] = shift(second, ys, -SHIFTS[n])
    part_a, part_b = pack(near_a, near_b)
    def turn(value, axes, d):
        pairs = [(2 * i + c, 2 * ((i + d - 2 * d * c) % 4) + c) for i in range(4) for c in range(2)]
        return lax.ppermute(value, (*axes, "c"), pairs)

    a_up, b_down = turn(part_a, ("y",), 1), turn(part_b, xs, -1)
    a_down, b_up = turn(part_a, ("y",), -1), turn(part_b, xs, 1)
    qq, *state = attend(info, tables[0], lists[0], (q_own, q_other), None, [part_a, part_b], False, 4)
    a_up, b_down, qq, state = lax.optimization_barrier((a_up, b_down, qq, state))
    a_far, b_far = turn(a_up, ("y",), 1), turn(b_down, xs, -1)
    state = attend(info, tables[1], lists[1], None, [qq, *state], [a_up, a_down, b_up, b_down], False, 8)
    o_own, o_other, lse_own, lse_other = attend(
        info, tables[2], lists[2], None, [qq, *state], [a_far, b_far], True, 4)

    o_got = lax.ppermute(o_other, "c", swap)
    lse_got = lax.ppermute(lse_other, "c", swap)
    a, b = lse_own.reshape(8, 2, 1, TILE), lse_got.reshape(8, 2, 1, TILE)
    most = jnp.maximum(a, b)
    wa, wb = jnp.exp2(a - most), jnp.exp2(b - most)
    o = (o_own.astype(jnp.float32) * wa + o_got.astype(jnp.float32) * wb) / (wa + wb)
    back = lax.all_to_all(o.astype(jnp.bfloat16), "z", split_axis=0, concat_axis=0, tiled=True)
    return back.reshape(4, 2, 2, HD, TILE).transpose(4, 1, 0, 2, 3).reshape(TILE, 16 * HD)


def solution(mesh):
    fine = Mesh(mesh.devices.reshape(SIZES), AXES)
    spec = P(AXES, None)
    return jax.shard_map(
        shards, mesh=fine, in_specs=(spec, spec, spec, P()), out_specs=spec, check_vma=False
    )
```
